256 devices in a mesh: section: 16 (over z, core), req: 16 (over y, x).
Axes of the slice: x: 4, y: 4, z: 8, core: 2. Of those that a mesh axis runs over, the one named last changes fastest.
Arguments:
- latents: bfloat16 [128, 3072], P('req'), may hold values from -6 to 6
- patch_route: int32 [128], replicated, may hold values from 0 to 127, each once
- request_len: int32 [16], replicated, may hold values from 1 to 32, 128 in all
- span_order: int32 [2], replicated, may hold values from 0 to 1, each once
- modulation: float32 [16, 16, 3, 3072], P('section'), may hold values from -4 to 4
- w_qkv: bfloat16 [16, 3072, 16, 384], P('section', None, 'req'), may hold values from -0.109375 to 0.109375
- w_mlp_in: bfloat16 [16, 3072, 6144], P('section', None, 'req'), may hold values from -0.109375 to 0.109375
- w_out_attn: bfloat16 [16, 16, 128, 3072], P('section', 'req'), may hold values from -0.0625 to 0.0625
- w_out_mlp: bfloat16 [16, 6144, 3072], P('section', 'req'), may hold values from -0.0625 to 0.0625
- stale_kv: bfloat16 [16, 128, 16, 256], P('section', None, 'req'), may hold values from -160 to 160
Outputs:
- denoised: bfloat16 [128, 3072], P('req', 'section')
The draws below stay inside these ranges and needn't reach their ends.
All inputs are finite; a program needn't handle non-finite values.
Results may differ from the reference program's by a relative error of at most 0.04.
Values may be sent and summed in bfloat16 or wider, within the bound.
No kernel may reach another device: no remote copies, remote signals or barrier semaphores. Data moves between devices by JAX's collectives and lax.ppermute only.
A program may use at most 64 MiB of HBM per device.

```python
import math
import jax
import jax.numpy as jnp
import numpy as np
from jax import lax

D = 3072
HEADS = 16
HD = 128
MLP = 6144
PATCHES = 128
SPANS = 2
REQS = 16
MOST = 32
SECTIONS = 16
N_REQ = 16


def draw_stale_kv(key, part):
    key = jax.random.fold_in(key, 7)
    shape = (SECTIONS, PATCHES, HEADS, 2 * HD)
    base = jnp.clip(jax.random.normal(key, shape, jnp.float32), -4.0, 4.0)
    return base.astype(jnp.bfloat16)


def steps_of(key, shape, shards, smallest, high):
    def one(dim, shards_of):
        steps = jax.random.uniform(jax.random.fold_in(jax.random.fold_in(key, 6), dim), (shards_of,), jnp.float32, smallest / len(shards), high / len(shards))
        return jnp.repeat(jnp.exp(steps), shape[dim] // shards_of).reshape((-1,) + (1,) * (len(shape) - dim - 1))

    factor_of = one(*shards[0])
    for cut in shards[1:]:
        factor_of = factor_of * one(*cut)
    return factor_of


def profile(count, total, most, skew):
    portions = [(1 << 20) // math.isqrt(standing ** skew) + 1 for standing in range(2, count + 1)]
    surplus, counts = total - most - (count - 1), [1] * (count - 1)
    while surplus > 0:
        movable = [i for i in range(count - 1) if counts[i] < most]
        mass, left = sum([portions[i] for i in movable]), surplus
        for i in movable:
            addition = min(most - counts[i], max(1, left * portions[i] // mass), surplus)
            counts[i] = counts[i] + addition
            surplus = surplus - addition
    return np.array([most] + counts)


def ragged(own_key, number_of, total, reach, lean):
    if number_of == 2:
        one = jax.random.randint(own_key, (), max(1, total - reach), min(reach, total - 1) + 1)
        return jnp.stack([one, total - one])
    sizes = jnp.asarray(profile(number_of, total, reach, lean), jnp.int32)
    couples = (number_of - 1) // 2
    source_of, taker = sizes[1:1 + 2 * couples:2], sizes[2:2 + 2 * couples:2]
    margin = jnp.minimum(source_of - 1, reach - taker)
    moved = jax.random.randint(jax.random.fold_in(own_key, 1), (couples,), 0, 1 << 20) % (margin + 1)
    sizes = sizes.at[1:1 + 2 * couples:2].set(source_of - moved).at[2:2 + 2 * couples:2].set(taker + moved)
    return sizes[jax.random.permutation(jax.random.fold_in(own_key, 2), number_of)]


def scatter_about(key, extent, scale, most, shards=(), held_as=jnp.bfloat16):
    values = jax.random.normal(key, extent, jnp.float32) * scale
    if len(shards) > 0:
        values = steps_of(key, extent, shards, -0.22, 0.18) * values
    return jnp.clip(values, min=-most, max=most).astype(held_as)


def setup_inputs(seed: int = 0) -> dict:
    keys = jax.random.split(jax.random.key(seed), 11)
    return {
        "latents": scatter_about(keys[0], (PATCHES, D), 1.0, 6.0, ((0, 16),)),
        "patch_route": jax.random.permutation(keys[1], PATCHES).astype(jnp.int32),
        "request_len": ragged(keys[2], REQS, PATCHES, MOST, 2).astype(jnp.int32),
        "span_order": jax.random.permutation(keys[3], SPANS).astype(jnp.int32),
        "modulation": scatter_about(keys[4], (SECTIONS, REQS, 3, D), 0.7, 4.0, ((0, 16),), jnp.float32),
        "w_qkv": scatter_about(keys[5], (SECTIONS, D, HEADS, 3 * HD), D ** -0.5, 0.109375, ((0, 16), (2, 16))),
        "w_mlp_in": scatter_about(keys[6], (SECTIONS, D, MLP), D ** -0.5, 0.109375, ((0, 16), (2, 16))),
        "w_out_attn": scatter_about(keys[7], (SECTIONS, HEADS, HD, D), (HEADS * HD + MLP) ** -0.5, 0.0625, ((0, 16), (1, 16))),
        "w_out_mlp": scatter_about(keys[8], (SECTIONS, MLP, D), (HEADS * HD + MLP) ** -0.5, 0.0625, ((0, 16), (1, 16))),
        "stale_kv": draw_stale_kv(jax.random.fold_in(keys[10], 71), 0),
    }


def layer_norm(values):
    row_mean = lax.optimization_barrier(jnp.mean(values, axis=-1, keepdims=True))
    centered = values - row_mean
    row_var = lax.optimization_barrier(jnp.mean(centered * centered, axis=-1, keepdims=True))
    return centered * lax.rsqrt(row_var + 1e-06)

def gelu_tanh(values):
    return 0.5 * values * (1.0 + jnp.tanh(0.7978845608028654 * (values + 0.044715 * values * values * values)))

def reference(latents, patch_route, request_len, span_order, modulation, w_qkv, w_mlp_in, w_out_attn, w_out_mlp, stale_kv):
    span_rows = PATCHES // SPANS
    heads_dev = HEADS // N_REQ
    mlp_dev = MLP // N_REQ
    starts = jnp.cumsum(request_len) - request_len
    patch_ids = jnp.arange(PATCHES, dtype=jnp.int32)
    owner_req = lax.optimization_barrier(jnp.sum((patch_ids[:, None] >= starts[None, :]).astype(jnp.int32), axis=1)) - 1
    seq_req = owner_req[patch_route]
    hidden = latents[patch_route]
    req_ids = jnp.arange(REQS, dtype=jnp.int32)
    for section_num in range(SECTIONS):
        mod_table = modulation[section_num].reshape(REQS, 3 * D)
        qkv_weight = w_qkv[section_num].reshape(D, HEADS * 3 * HD)
        mlp_weight = w_mlp_in[section_num]
        attn_out_weight = w_out_attn[section_num].reshape(N_REQ, heads_dev * HD, D).astype(jnp.float32)
        mlp_out_weight = w_out_mlp[section_num].reshape(N_REQ, mlp_dev, D).astype(jnp.float32)

        def block_step(carry, span_id):
            hidden_now, kv_cache = carry
            first_row = (span_id * span_rows).astype(jnp.int32)
            current = lax.dynamic_slice_in_dim(hidden_now, first_row, span_rows, 0)
            row_req = lax.dynamic_slice_in_dim(seq_req, first_row, span_rows, 0)
            onehot = (row_req[:, None] == req_ids[None, :]).astype(jnp.float32)
            mod_rows = jnp.dot(onehot, mod_table, precision=lax.Precision.HIGHEST).reshape(span_rows, 3, D)
            normed = (layer_norm(current.astype(jnp.float32)) * (1.0 + mod_rows[:, 1]) + mod_rows[:, 0]).astype(jnp.bfloat16)
            qkv_rows = jnp.dot(normed, qkv_weight, preferred_element_type=jnp.float32).reshape(span_rows, HEADS, 3 * HD)
            query_rows = qkv_rows[:, :, :HD].astype(jnp.bfloat16)
            fresh_kv = qkv_rows[:, :, HD:].astype(jnp.bfloat16)
            kv_cache = lax.dynamic_update_slice_in_dim(kv_cache, fresh_kv, first_row, 0)
            key_rows = kv_cache[:, :, :HD].astype(jnp.float32)
            value_rows = kv_cache[:, :, HD:].astype(jnp.float32)
            scores = jnp.einsum('chd,phd->hcp', query_rows.astype(jnp.float32), key_rows) / jnp.sqrt(jnp.float32(HD))
            same_req = row_req[:, None] == seq_req[None, :]
            scores = jnp.where(same_req[None], scores, -jnp.inf)
            row_top = lax.optimization_barrier(jnp.max(scores, axis=-1, keepdims=True))
            weights = jnp.exp(scores - row_top)
            weight_sum = lax.optimization_barrier(jnp.sum(weights, axis=-1, keepdims=True))
            attention = (weights / weight_sum).astype(jnp.bfloat16)
            attended = jnp.einsum('hcp,phd->chd', attention.astype(jnp.float32), value_rows).astype(jnp.bfloat16)
            mlp_act = gelu_tanh(jnp.dot(normed, mlp_weight, preferred_element_type=jnp.float32)).astype(jnp.bfloat16)
            partial_value = jnp.einsum('crk,rkd->rcd', attended.reshape(span_rows, N_REQ, heads_dev * HD).astype(jnp.float32), attn_out_weight)
            partial_value = partial_value + jnp.einsum('crk,rkd->rcd', mlp_act.reshape(span_rows, N_REQ, mlp_dev).astype(jnp.float32), mlp_out_weight)
            rounded = lax.optimization_barrier(partial_value.astype(jnp.bfloat16))
            branch = lax.optimization_barrier(jnp.sum(rounded.astype(jnp.float32), axis=0))
            updated = (current.astype(jnp.float32) + mod_rows[:, 2] * branch).astype(jnp.bfloat16)
            hidden_now = lax.dynamic_update_slice_in_dim(hidden_now, updated, first_row, 0)
            return ((hidden_now, kv_cache), jnp.int32(0))
        (hidden, last_cache), unused = lax.scan(block_step, (hidden, stale_kv[section_num]), span_order)
    return jnp.zeros_like(latents).at[patch_route].set(hidden)
```

```python
import jax
import jax.numpy as jnp
from jax import lax
from jax.sharding import PartitionSpec as P

AXES = ("section", "req")
BF16 = jnp.bfloat16


def gelu_tanh(values):
    return (
        0.5
        * values
        * (1.0 + jnp.tanh(0.7978845608028654 * (values + 0.044715 * values * values * values)))
    )


def layer_norm(values):
    row_mean = jnp.mean(values, axis=-1, keepdims=True)
    centered = values - row_mean
    row_var = jnp.mean(centered * centered, axis=-1, keepdims=True)
    return centered * lax.rsqrt(row_var + 1e-06)


def shards(
    latents,
    patch_route,
    request_len,
    span_order,
    modulation,
    w_qkv,
    w_mlp_in,
    w_out_attn,
    w_out_mlp,
    stale_kv,
):
    section_count = lax.axis_size("section")
    req_count = lax.axis_size("req")
    section_index = lax.axis_index("section")
    req_index = lax.axis_index("req")
    patches = patch_route.shape[0]
    span_rows = patches // span_order.shape[0]
    own_rows, width = latents.shape
    req_total = request_len.shape[0]
    head_dim = w_qkv.shape[3] // 3

    starts = jnp.cumsum(request_len) - request_len
    rows = jnp.arange(patches, dtype=jnp.int32)
    row_req = jnp.sum((rows[:, None] >= starts[None, :]).astype(jnp.int32), axis=1) - 1
    at_position = rows[:, None] == patch_route[None, :]
    positions = jnp.sum(jnp.where(at_position, rows[None, :], 0), axis=1)
    is_first = positions // span_rows == span_order[0]
    same_req = row_req[:, None] == row_req[None, :]
    from_stale = is_first[:, None] & ~is_first[None, :]
    stale = jnp.dot(
        at_position.astype(BF16), stale_kv[0, :, 0], preferred_element_type=jnp.float32
    ).astype(BF16)
    owned_req = lax.dynamic_slice_in_dim(row_req, req_index * own_rows, own_rows, 0)
    onehot = (owned_req[:, None] == jnp.arange(req_total, dtype=jnp.int32)[None, :]).astype(
        jnp.float32
    )
    mod = jnp.einsum("cr,rkd->kcd", onehot, modulation[0], precision=lax.Precision.HIGHEST)

    qkv_weight, mlp_weight = w_qkv[0, :, 0], w_mlp_in[0]
    attn_out_weight, mlp_out_weight = w_out_attn[0, 0], w_out_mlp[0]

    def heads_and_units(normed):
        qkv_rows = jnp.dot(normed, qkv_weight, preferred_element_type=jnp.float32).astype(BF16)
        query, key, value = (
            qkv_rows[:, :head_dim],
            qkv_rows[:, head_dim : 2 * head_dim],
            qkv_rows[:, 2 * head_dim :],
        )
        against_fresh = jnp.dot(query, key.T, preferred_element_type=jnp.float32)
        against_stale = jnp.dot(query, stale[:, :head_dim].T, preferred_element_type=jnp.float32)
        scores = jnp.where(from_stale, against_stale, against_fresh) / jnp.sqrt(
            jnp.float32(head_dim)
        )
        scores = jnp.where(same_req, scores, -jnp.inf)
        row_top = jnp.max(scores, axis=-1, keepdims=True)
        exps = jnp.exp(scores - row_top)
        attention = (exps / jnp.sum(exps, axis=-1, keepdims=True)).astype(BF16)
        none = jnp.zeros_like(attention)
        attended = jnp.dot(
            jnp.where(from_stale, none, attention), value, preferred_element_type=jnp.float32
        ) + jnp.dot(
            jnp.where(from_stale, attention, none),
            stale[:, head_dim:],
            preferred_element_type=jnp.float32,
        )
        mlp_act = gelu_tanh(
            jnp.dot(normed, mlp_weight, preferred_element_type=jnp.float32)
        ).astype(BF16)
        partial_value = jnp.dot(
            attended.astype(BF16), attn_out_weight, preferred_element_type=jnp.float32
        ) + jnp.dot(mlp_act, mlp_out_weight, preferred_element_type=jnp.float32)
        return partial_value.astype(BF16)

    def exchange(value):
        return lax.all_to_all(value, "req", split_axis=0, concat_axis=0, tiled=True)

    def section_step(current):
        normed = (layer_norm(current.astype(jnp.float32)) * (1.0 + mod[1]) + mod[0]).astype(BF16)
        everyone = exchange(jnp.broadcast_to(normed[None], (req_count, own_rows, width)))
        partial_value = heads_and_units(everyone.reshape(patches, width))
        shares = exchange(partial_value.reshape(req_count, own_rows, width))
        branch = jnp.sum(shares.astype(jnp.float32), axis=0)
        return (current.astype(jnp.float32) + mod[2] * branch).astype(BF16)

    onward = [(i, i + req_count) for i in range((section_count - 1) * req_count)]

    def advance(turn, current):
        current = lax.cond(section_index == turn, section_step, lambda values: values, current)
        arrived = lax.ppermute(current, AXES, onward)
        return jnp.where(section_index == turn + 1, arrived, current)

    current = lax.fori_loop(0, section_count, advance, latents)
    pieces = current.reshape(own_rows, section_count, width // section_count).swapaxes(0, 1)
    pieces = lax.all_to_all(pieces, "section", split_axis=0, concat_axis=0, tiled=True)
    return pieces[section_count - 1]


def solution(mesh):
    in_specs = (
        P("req", None),
        P(),
        P(),
        P(),
        P("section", None, None, None),
        P("section", None, "req", None),
        P("section", None, "req"),
        P("section", "req", None, None),
        P("section", "req", None),
        P("section", None, "req", None),
    )
    out_specs = P("req", "section")
    return jax.shard_map(shards, mesh=mesh, in_specs=in_specs, out_specs=out_specs, check_vma=False)
```

```python
import functools

import jax
import jax.numpy as jnp
from jax import lax
from jax.experimental import pallas as pl
from jax.experimental.pallas import tpu as pltpu
from jax.sharding import PartitionSpec as P

AXES = ("section", "req")
BF16 = jnp.bfloat16
WIDTH_CUTS = 4
TILE = 16
VMEM = pl.BlockSpec(memory_space=pltpu.VMEM)
ANY = pl.BlockSpec(memory_space=pl.ANY)
PARAMS = pltpu.CompilerParams(vmem_limit_bytes=16 * 1024 * 1024)


def gelu_tanh(values):
    return (
        0.5
        * values
        * (1.0 + jnp.tanh(0.7978845608028654 * (values + 0.044715 * values * values * values)))
    )


def block_kernel(
    head_dim,
    rows_ref,
    qkv_ref,
    mlp_ref,
    attn_out_ref,
    mlp_out_ref,
    stale_ref,
    from_stale_ref,
    bias_ref,
    out_ref,
):
    qkv = jnp.dot(rows_ref[...], qkv_ref[...], preferred_element_type=jnp.float32).astype(BF16)
    query, key, value = (
        qkv[:, :head_dim],
        qkv[:, head_dim : 2 * head_dim],
        qkv[:, 2 * head_dim :],
    )
    across = (((1,), (1,)), ((), ()))
    against_fresh = lax.dot_general(query, key, across, preferred_element_type=jnp.float32)
    against_stale = lax.dot_general(
        query, stale_ref[:, :head_dim], across, preferred_element_type=jnp.float32
    )
    from_stale = from_stale_ref[...] > 0.0
    scores = jnp.where(from_stale, against_stale, against_fresh) / jnp.sqrt(
        jnp.float32(head_dim)
    )
    scores = scores + bias_ref[...]
    exps = jnp.exp(scores - jnp.max(scores, axis=-1, keepdims=True))
    attention = exps / jnp.sum(exps, axis=-1, keepdims=True)
    attended = jnp.dot(
        jnp.where(from_stale, 0.0, attention).astype(BF16),
        value,
        preferred_element_type=jnp.float32,
    ) + jnp.dot(
        jnp.where(from_stale, attention, 0.0).astype(BF16),
        stale_ref[:, head_dim:],
        preferred_element_type=jnp.float32,
    )
    attended = attended.astype(BF16)
    mlp_act = gelu_tanh(
        jnp.dot(rows_ref[...], mlp_ref[...], preferred_element_type=jnp.float32)
    ).astype(BF16)
    cols = out_ref.shape[1] // WIDTH_CUTS
    for cut in range(WIDTH_CUTS):
        span = slice(cut * cols, (cut + 1) * cols)
        out_ref[:, span] = (
            jnp.dot(attended, attn_out_ref[:, span], preferred_element_type=jnp.float32)
            + jnp.dot(mlp_act, mlp_out_ref[:, span], preferred_element_type=jnp.float32)
        ).astype(BF16)


def spread_normed(current, mod_ref, out_ref):
    row_mean = jnp.mean(current, axis=-1, keepdims=True)
    centered = current - row_mean
    row_var = jnp.mean(centered * centered, axis=-1, keepdims=True)
    normed = centered * lax.rsqrt(row_var + 1e-06) * (1.0 + mod_ref[1]) + mod_ref[0]
    twice = jnp.concatenate([normed, normed], axis=0).astype(BF16)
    for first in range(0, out_ref.shape[0], TILE):
        out_ref[first : first + TILE, :] = twice


def summed(shares_ref, current_ref, mod_ref):
    branch = shares_ref[:TILE, :].astype(jnp.float32)
    for first in range(TILE, shares_ref.shape[0], TILE):
        branch = branch + shares_ref[first : first + TILE, :].astype(jnp.float32)
    branch = branch[: TILE // 2] + branch[TILE // 2 :]
    return (current_ref[...].astype(jnp.float32) + mod_ref[2] * branch).astype(BF16)


def norm_kernel(current_ref, mod_ref, *refs):
    spread_normed(current_ref[...].astype(jnp.float32), mod_ref, refs[-1])


def sum_kernel(shares_ref, current_ref, mod_ref, out_ref):
    out_ref[...] = summed(shares_ref, current_ref, mod_ref)


def shards(
    latents,
    patch_route,
    request_len,
    span_order,
    modulation,
    w_qkv,
    w_mlp_in,
    w_out_attn,
    w_out_mlp,
    stale_kv,
):
    section_count = lax.axis_size("section")
    req_count = lax.axis_size("req")
    section_index = lax.axis_index("section")
    req_index = lax.axis_index("req")
    patches = patch_route.shape[0]
    span_rows = patches // span_order.shape[0]
    own_rows, width = latents.shape
    req_total = request_len.shape[0]
    head_dim = w_qkv.shape[3] // 3

    starts = jnp.cumsum(request_len) - request_len
    rows = jnp.arange(patches, dtype=jnp.int32)
    row_req = jnp.sum((rows[:, None] >= starts[None, :]).astype(jnp.int32), axis=1) - 1
    at_position = rows[:, None] == patch_route[None, :]
    positions = jnp.sum(jnp.where(at_position, rows[None, :], 0), axis=1)
    is_first = positions // span_rows == span_order[0]
    same_req = row_req[:, None] == row_req[None, :]
    from_stale = (is_first[:, None] & ~is_first[None, :]).astype(jnp.float32)
    bias = jnp.where(same_req, 0.0, -jnp.inf).astype(jnp.float32)
    stale = jnp.dot(
        at_position.astype(BF16), stale_kv[0, :, 0], preferred_element_type=jnp.float32
    ).astype(BF16)
    owned_req = lax.dynamic_slice_in_dim(row_req, req_index * own_rows, own_rows, 0)
    onehot = (owned_req[:, None] == jnp.arange(req_total, dtype=jnp.int32)[None, :]).astype(
        jnp.float32
    )
    mod = jnp.einsum("cr,rkd->kcd", onehot, modulation[0], precision=lax.Precision.HIGHEST)
    held = lax.optimization_barrier((mod, stale, from_stale, bias))
    mod, stale, from_stale, bias = held
    weights = (w_qkv[0, :, 0], w_mlp_in[0], w_out_attn[0, 0], w_out_mlp[0])

    all_rows = jax.ShapeDtypeStruct((patches, width), BF16)
    own = jax.ShapeDtypeStruct((own_rows, width), BF16)
    norm = pl.pallas_call(
        norm_kernel,
        out_shape=all_rows,
        in_specs=[VMEM] * 2 + [ANY] * 4,
        out_specs=VMEM,
        compiler_params=PARAMS,
        name="spread_normed",
    )
    heads_and_units = pl.pallas_call(
        functools.partial(block_kernel, head_dim),
        out_shape=all_rows,
        in_specs=[VMEM] * 8,
        out_specs=VMEM,
        compiler_params=PARAMS,
        name="heads_and_units",
    )
    add_shares = pl.pallas_call(
        sum_kernel,
        out_shape=own,
        in_specs=[VMEM] * 3,
        out_specs=VMEM,
        compiler_params=PARAMS,
        name="add_shares",
    )

    def exchange(value):
        value = value.reshape(req_count, own_rows, width)
        value = lax.all_to_all(value, "req", split_axis=0, concat_axis=0, tiled=True)
        return value.reshape(patches, width)

    def section_step(current):
        everyone = exchange(norm(current, mod, *weights))
        partial_value = heads_and_units(
            everyone,
            *[pltpu.with_memory_space_constraint(weight, pltpu.VMEM) for weight in weights],
            stale,
            from_stale,
            bias,
        )
        return add_shares(exchange(partial_value), current, mod)

    onward = [(i, i + req_count) for i in range((section_count - 1) * req_count)]

    def at_turn(turn, current):
        return lax.cond(section_index == turn, section_step, lambda values: values, current)

    def advance(turn, current):
        return lax.ppermute(at_turn(turn, current), AXES, onward)

    current = lax.fori_loop(0, section_count - 1, advance, latents)
    current = at_turn(section_count - 1, current)
    pieces = current.reshape(own_rows, section_count, width // section_count).swapaxes(0, 1)
    pieces = lax.all_to_all(pieces, "section", split_axis=0, concat_axis=0, tiled=True)
    return pieces[section_count - 1]


def solution(mesh):
    in_specs = (
        P("req", None),
        P(),
        P(),
        P(),
        P("section", None, None, None),
        P("section", None, "req", None),
        P("section", None, "req"),
        P("section", "req", None, None),
        P("section", "req", None),
        P("section", None, "req", None),
    )
    out_specs = P("req", "section")
    return jax.shard_map(shards, mesh=mesh, in_specs=in_specs, out_specs=out_specs, check_vma=False)
```

```python
import functools

import jax
import jax.numpy as jnp
from jax import lax
from jax.experimental import pallas as pl
from jax.experimental.pallas import tpu as pltpu
from jax.sharding import PartitionSpec as P

AXES = ("section", "req")
BF16 = jnp.bfloat16
WIDTH_CUTS = 4
TILE = 16
VMEM = pl.BlockSpec(memory_space=pltpu.VMEM)
ANY = pl.BlockSpec(memory_space=pl.ANY)
PARAMS = pltpu.CompilerParams(vmem_limit_bytes=16 * 1024 * 1024)


def gelu_tanh(values):
    return (
        0.5
        * values
        * (1.0 + jnp.tanh(0.7978845608028654 * (values + 0.044715 * values * values * values)))
    )


def prepare_kernel(
    req_ref,
    span_hbm,
    route_hbm,
    len_hbm,
    modulation_hbm,
    stale_hbm,
    aux_ref,
    mod_ref,
    span_ref,
    route_ref,
    len_ref,
    modulation_ref,
    stale_ref,
    sems,
):
    moves = (
        (span_hbm, span_ref),
        (route_hbm, route_ref),
        (len_hbm, len_ref),
        (modulation_hbm, modulation_ref),
        (stale_hbm, stale_ref),
    )
    copies = [
        pltpu.make_async_copy(source, target, sems.at[i])
        for i, (source, target) in enumerate(moves)
    ]
    for copy in copies:
        copy.start()
    for copy in copies:
        copy.wait()
    patches = route_ref.shape[1]
    reqs = len_ref.shape[1]
    span_rows = patches // span_ref.shape[0]
    own_rows = mod_ref.shape[1]
    f32 = jnp.float32

    def down(rows, cols):
        return lax.broadcasted_iota(jnp.int32, (rows, cols), 0)

    def along(rows, cols):
        return lax.broadcasted_iota(jnp.int32, (rows, cols), 1)

    def total(mask, values, axis):
        return jnp.sum(jnp.where(mask, values, 0.0), axis=axis, keepdims=True)

    lens = jnp.broadcast_to(len_ref[...].astype(f32), (reqs, reqs))
    lens_down = total(down(reqs, reqs) == along(reqs, reqs), lens, 1)
    starts_along = total(down(reqs, reqs) < along(reqs, reqs), lens_down, 0)
    starts_down = total(along(reqs, reqs) < down(reqs, reqs), lens, 1)
    req_down = total(down(patches, reqs).astype(f32) >= starts_along, 1.0, 1) - 1.0
    req_along = total(along(reqs, patches).astype(f32) >= starts_down, 1.0, 0) - 1.0
    route = jnp.broadcast_to(route_ref[...], (patches, patches))
    square_down, square_along = down(patches, patches), along(patches, patches)
    at_position = square_down == route
    route_down = total(square_down == square_along, route.astype(f32), 1)
    position_down = total(at_position, square_along.astype(f32), 1)
    position_along = total(route_down == square_along.astype(f32), square_down.astype(f32), 0)
    first_row = (span_ref[0] * span_rows).astype(f32)

    def in_first(position):
        return (position >= first_row) & (position < first_row + span_rows)

    from_stale = jnp.where(in_first(position_down), 1.0, 0.0) * jnp.where(
        in_first(position_along), 0.0, 1.0
    )
    kind = jnp.where(req_down == req_along, 1.0 + from_stale, 0.0)
    stale_cols = stale_ref.shape[1]
    aux_ref[:, :stale_cols] = jnp.dot(
        jnp.where(at_position, 1.0, 0.0).astype(BF16),
        stale_ref[...],
        preferred_element_type=f32,
    ).astype(BF16)
    aux_ref[:, stale_cols:] = kind.astype(BF16)
    own = (down(own_rows, reqs) + req_ref[0] * own_rows).astype(f32)
    own_req = total(own >= starts_along, 1.0, 1) - 1.0
    for part in range(mod_ref.shape[0]):
        chosen = jnp.zeros(mod_ref.shape[1:], f32)
        for req in range(reqs):
            chosen = chosen + jnp.where(own_req == req, 1.0, 0.0) * modulation_ref[
                part, req : req + 1, :
            ]
        mod_ref[part] = chosen


def pack_kernel(qkv_ref, mlp_ref, attn_out_ref, mlp_out_ref, packed_ref, sems):
    width, qkv_cols = qkv_ref.shape
    head_dim, units = attn_out_ref.shape[0], mlp_out_ref.shape[0]
    cols = packed_ref.shape[1]
    moves = [
        (qkv_ref, packed_ref.at[pl.ds(0, width), pl.ds(0, qkv_cols)]),
        (mlp_ref, packed_ref.at[pl.ds(0, width), pl.ds(qkv_cols, units)]),
    ]
    for cut in range(width // cols):
        first = width + cut * (head_dim + units)
        span = pl.ds(cut * cols, cols)
        moves += [
            (attn_out_ref.at[:, span], packed_ref.at[pl.ds(first, head_dim), :]),
            (mlp_out_ref.at[:, span], packed_ref.at[pl.ds(first + head_dim, units), :]),
        ]
    copies = [
        pltpu.make_async_copy(source, target, sems.at[i])
        for i, (source, target) in enumerate(moves)
    ]
    for copy in copies:
        copy.start()
    for copy in copies:
        copy.wait()


def attend(qkv, aux_ref):
    head_dim = qkv.shape[1] // 3
    stale_cols = 2 * head_dim
    kind = aux_ref[:, stale_cols:]
    query, key, value = (
        qkv[:, :head_dim],
        qkv[:, head_dim : 2 * head_dim],
        qkv[:, 2 * head_dim :],
    )
    across = (((1,), (1,)), ((), ()))
    against_fresh = lax.dot_general(query, key, across, preferred_element_type=jnp.float32)
    against_stale = lax.dot_general(
        query, aux_ref[:, :head_dim], across, preferred_element_type=jnp.float32
    )
    kind = kind.astype(jnp.float32)
    from_stale = kind > 1.5
    scores = jnp.where(from_stale, against_stale, against_fresh) / jnp.sqrt(
        jnp.float32(head_dim)
    )
    scores = jnp.where(kind > 0.5, scores, -jnp.inf)
    exps = jnp.exp(scores - jnp.max(scores, axis=-1, keepdims=True))
    attention = exps / jnp.sum(exps, axis=-1, keepdims=True)
    attended = jnp.dot(
        jnp.where(from_stale, 0.0, attention).astype(BF16),
        value,
        preferred_element_type=jnp.float32,
    ) + jnp.dot(
        jnp.where(from_stale, attention, 0.0).astype(BF16),
        aux_ref[:, head_dim:stale_cols],
        preferred_element_type=jnp.float32,
    )
    return attended.astype(BF16)


def block_kernel(
    rows_ref,
    qkv_ref,
    mlp_ref,
    attn_out_ref,
    mlp_out_ref,
    aux_ref,
    out_ref,
):
    qkv = jnp.dot(rows_ref[...], qkv_ref[...], preferred_element_type=jnp.float32).astype(BF16)
    attended = attend(qkv, aux_ref)
    mlp_act = gelu_tanh(
        jnp.dot(rows_ref[...], mlp_ref[...], preferred_element_type=jnp.float32)
    ).astype(BF16)
    cols = out_ref.shape[1] // WIDTH_CUTS
    for cut in range(WIDTH_CUTS):
        span = slice(cut * cols, (cut + 1) * cols)
        out_ref[:, span] = (
            jnp.dot(attended, attn_out_ref[:, span], preferred_element_type=jnp.float32)
            + jnp.dot(mlp_act, mlp_out_ref[:, span], preferred_element_type=jnp.float32)
        ).astype(BF16)


def packed_block_kernel(qkv_cols, rows_ref, packed_ref, aux_ref, out_ref):
    width = rows_ref.shape[1]
    cols = packed_ref.shape[1]
    cuts = width // cols
    depth = (packed_ref.shape[0] - width) // cuts
    total = jnp.dot(
        rows_ref[...], packed_ref[:width, :], preferred_element_type=jnp.float32
    )
    attended = attend(total[:, :qkv_cols].astype(BF16), aux_ref)
    mlp_act = gelu_tanh(total[:, qkv_cols:]).astype(BF16)
    inner = jnp.concatenate([attended, mlp_act], axis=1)
    for cut in range(cuts):
        first = width + cut * depth
        out_ref[:, cut * cols : (cut + 1) * cols] = jnp.dot(
            inner, packed_ref[first : first + depth, :], preferred_element_type=jnp.float32
        ).astype(BF16)


def spread_normed(current, mod_ref, out_ref):
    row_mean = jnp.mean(current, axis=-1, keepdims=True)
    centered = current - row_mean
    row_var = jnp.mean(centered * centered, axis=-1, keepdims=True)
    normed = centered * lax.rsqrt(row_var + 1e-06) * (1.0 + mod_ref[1]) + mod_ref[0]
    twice = jnp.concatenate([normed, normed], axis=0).astype(BF16)
    for first in range(0, out_ref.shape[0], TILE):
        out_ref[first : first + TILE, :] = twice


def summed(shares_ref, current_ref, mod_ref):
    branch = shares_ref[:TILE, :].astype(jnp.float32)
    for first in range(TILE, shares_ref.shape[0], TILE):
        branch = branch + shares_ref[first : first + TILE, :].astype(jnp.float32)
    branch = branch[: TILE // 2] + branch[TILE // 2 :]
    return (current_ref[...].astype(jnp.float32) + mod_ref[2] * branch).astype(BF16)


def nothing_kernel(*refs):
    pass


def keep_kernel(*refs):
    for source, target in zip(refs[: len(refs) // 2], refs[len(refs) // 2 :]):
        target[...] = source[...]


def norm_kernel(current_ref, mod_ref, *refs):
    spread_normed(current_ref[...].astype(jnp.float32), mod_ref, refs[-1])


def sum_kernel(shares_ref, current_ref, mod_ref, out_ref):
    out_ref[...] = summed(shares_ref, current_ref, mod_ref)


def shards(
    latents,
    patch_route,
    request_len,
    span_order,
    modulation,
    w_qkv,
    w_mlp_in,
    w_out_attn,
    w_out_mlp,
    stale_kv,
):
    section_count = lax.axis_size("section")
    req_count = lax.axis_size("req")
    section_index = lax.axis_index("section")
    req_index = lax.axis_index("req")
    patches = patch_route.shape[0]
    own_rows, width = latents.shape
    qkv_cols = w_qkv.shape[3]
    head_dim = w_out_attn.shape[2]
    units = w_mlp_in.shape[2]

    near = pl.BlockSpec(memory_space=pltpu.SMEM)
    operands = (
        span_order,
        patch_route.reshape(1, patches),
        request_len.reshape(1, -1),
        modulation[0].swapaxes(0, 1),
        stale_kv[0, :, 0],
    )
    aux, mod = pl.pallas_call(
        prepare_kernel,
        out_shape=(
            pltpu.VMEM((patches, 2 * head_dim + patches), BF16),
            pltpu.VMEM((3, own_rows, width), jnp.float32),
        ),
        in_specs=[near] + [ANY] * 5,
        out_specs=(VMEM, VMEM),
        scratch_shapes=[pltpu.SMEM(span_order.shape, span_order.dtype)]
        + [pltpu.VMEM(value.shape, value.dtype) for value in operands[1:]]
        + [pltpu.SemaphoreType.DMA((5,))],
        compiler_params=PARAMS,
        name="prepare",
    )(req_index.astype(jnp.int32).reshape(1), *operands)
    mod, aux = lax.optimization_barrier((mod, aux))
    own_weights = (w_qkv[0, :, 0], w_mlp_in[0], w_out_attn[0, 0], w_out_mlp[0])
    to_sibling = [
        (i, i + req_count)
        for i in range(2 * req_count, section_count * req_count)
        if i // req_count % 2 == 0
    ]
    packed_cols = qkv_cols + units
    pack = pl.pallas_call(
        pack_kernel,
        out_shape=jax.ShapeDtypeStruct(
            (width + width // packed_cols * (head_dim + units), packed_cols), BF16
        ),
        in_specs=[ANY] * 4,
        out_specs=VMEM,
        compiler_params=PARAMS,
        scratch_shapes=[pltpu.SemaphoreType.DMA((2 + 2 * (width // packed_cols),))],
        name="pack_weights",
    )

    def chip_sections(weights, aux, mod):
        own = (pack(*weights), aux, mod)
        return own[0], *(lax.ppermute(value, AXES, to_sibling) for value in own)

    def unused(function):
        def nothing(*values):
            shapes, tree = jax.tree.flatten(jax.eval_shape(function, *values))
            results = pl.pallas_call(
                nothing_kernel,
                out_shape=tuple(jax.ShapeDtypeStruct(v.shape, v.dtype) for v in shapes),
                out_specs=(ANY,) * len(shapes),
                name="unused",
            )()
            return jax.tree.unflatten(tree, results)

        return nothing

    all_rows = jax.ShapeDtypeStruct((patches, width), BF16)
    own = jax.ShapeDtypeStruct((own_rows, width), BF16)
    def norm(current, mod, *weights):
        return pl.pallas_call(
            norm_kernel,
            out_shape=all_rows,
            in_specs=[VMEM] * 2 + [ANY] * len(weights),
            out_specs=VMEM,
            compiler_params=PARAMS,
            name="spread_normed",
        )(current, mod, *weights)

    def heads_and_units(everyone, weights, aux):
        kernel = block_kernel
        if len(weights) == 1:
            kernel = functools.partial(packed_block_kernel, qkv_cols)
        return pl.pallas_call(
            kernel,
            out_shape=all_rows,
            in_specs=[VMEM] * (2 + len(weights)),
            out_specs=VMEM,
            compiler_params=PARAMS,
            name="heads_and_units",
        )(
            everyone,
            *[pltpu.with_memory_space_constraint(value, pltpu.VMEM) for value in weights],
            aux,
        )

    add_shares = pl.pallas_call(
        sum_kernel,
        out_shape=own,
        in_specs=[VMEM] * 3,
        out_specs=VMEM,
        compiler_params=PARAMS,
        name="add_shares",
    )

    def exchange(value):
        value = value.reshape(req_count, own_rows, width)
        value = lax.all_to_all(value, "req", split_axis=0, concat_axis=0, tiled=True)
        return value.reshape(patches, width)

    def one_section(current, *section):
        *weights, aux, mod = section
        everyone = exchange(norm(current, mod, *weights, aux))
        partial_value = heads_and_units(everyone, weights, aux)
        return add_shares(exchange(partial_value), current, mod)

    def when(section, current, held):
        return lax.cond(
            section_index == section, one_section, unused(one_section), current, *held
        )

    def hand_over(current, sections):
        pairs = [(a * req_count + i, b * req_count + i) for a, b in sections for i in range(req_count)]
        return lax.ppermute(current, AXES, pairs)

    def chip_turn(chip, current):
        current = when(2 * chip + 1, current, first_held)
        return when(2 * chip + 1, current, second_held)

    onward = [(section, section + 2) for section in range(1, section_count - 1, 2)]
    current = when(0, latents, (*own_weights, aux, mod))
    current = hand_over(current, [(0, 1)])
    current = when(1, current, (*own_weights, aux, mod))
    current = hand_over(current, onward)
    own_packed, *first_held = lax.cond(
        section_index >= 2, chip_sections, unused(chip_sections), own_weights, aux, mod
    )
    own_packed, first_packed = (
        jnp.where(section_index >= 2, value, jnp.zeros_like(value))
        for value in (own_packed, first_held[0])
    )
    small = pl.pallas_call(
        keep_kernel,
        out_shape=tuple(pltpu.VMEM(value.shape, value.dtype) for value in (aux, mod)),
        in_specs=[VMEM] * 2,
        out_specs=(VMEM, VMEM),
        compiler_params=PARAMS,
        name="keep",
    )(*first_held[1:])
    first_held = (first_packed, *small)
    second_held = (own_packed, aux, mod)
    last = section_count // 2 - 1
    current = lax.fori_loop(
        1, last, lambda chip, rows: hand_over(chip_turn(chip, rows), onward), current
    )
    current = chip_turn(last, current)
    pieces = current.reshape(own_rows, section_count, width // section_count).swapaxes(0, 1)
    pieces = lax.all_to_all(pieces, "section", split_axis=0, concat_axis=0, tiled=True)
    return pieces[section_count - 1]


def solution(mesh):
    in_specs = (
        P("req", None),
        P(),
        P(),
        P(),
        P("section", None, None, None),
        P("section", None, "req", None),
        P("section", None, "req"),
        P("section", "req", None, None),
        P("section", "req", None),
        P("section", None, "req", None),
    )
    out_specs = P("req", "section")
    return jax.shard_map(shards, mesh=mesh, in_specs=in_specs, out_specs=out_specs, check_vma=False)
```

```python
import functools

import jax
import jax.numpy as jnp
from jax import lax
from jax.experimental import pallas as pl
from jax.experimental.pallas import tpu as pltpu
from jax.sharding import PartitionSpec as P

AXES = ("section", "req")
BF16 = jnp.bfloat16
WIDTH_CUTS = 4
TILE = 16
VMEM = pl.BlockSpec(memory_space=pltpu.VMEM)
ANY = pl.BlockSpec(memory_space=pl.ANY)
LARGE = pltpu.CompilerParams(vmem_limit_bytes=58 * 1024 * 1024)
PARAMS = pltpu.CompilerParams(vmem_limit_bytes=16 * 1024 * 1024)


def gelu_tanh(values):
    return (
        0.5
        * values
        * (1.0 + jnp.tanh(0.7978845608028654 * (values + 0.044715 * values * values * values)))
    )


def prepare_kernel(
    req_ref,
    span_hbm,
    route_hbm,
    len_hbm,
    modulation_hbm,
    stale_hbm,
    aux_ref,
    mod_ref,
    span_ref,
    route_ref,
    len_ref,
    modulation_ref,
    stale_ref,
    sems,
):
    moves = (
        (span_hbm, span_ref),
        (route_hbm, route_ref),
        (len_hbm, len_ref),
        (modulation_hbm, modulation_ref),
        (stale_hbm, stale_ref),
    )
    copies = [
        pltpu.make_async_copy(source, target, sems.at[i])
        for i, (source, target) in enumerate(moves)
    ]
    for copy in copies:
        copy.start()
    for copy in copies:
        copy.wait()
    patches = route_ref.shape[1]
    reqs = len_ref.shape[1]
    span_rows = patches // span_ref.shape[0]
    own_rows = mod_ref.shape[1]
    f32 = jnp.float32

    def down(rows, cols):
        return lax.broadcasted_iota(jnp.int32, (rows, cols), 0)

    def along(rows, cols):
        return lax.broadcasted_iota(jnp.int32, (rows, cols), 1)

    def total(mask, values, axis):
        return jnp.sum(jnp.where(mask, values, 0.0), axis=axis, keepdims=True)

    lens = jnp.broadcast_to(len_ref[...].astype(f32), (reqs, reqs))
    lens_down = total(down(reqs, reqs) == along(reqs, reqs), lens, 1)
    starts_along = total(down(reqs, reqs) < along(reqs, reqs), lens_down, 0)
    starts_down = total(along(reqs, reqs) < down(reqs, reqs), lens, 1)
    req_down = total(down(patches, reqs).astype(f32) >= starts_along, 1.0, 1) - 1.0
    req_along = total(along(reqs, patches).astype(f32) >= starts_down, 1.0, 0) - 1.0
    route = jnp.broadcast_to(route_ref[...], (patches, patches))
    square_down, square_along = down(patches, patches), along(patches, patches)
    at_position = square_down == route
    route_down = total(square_down == square_along, route.astype(f32), 1)
    position_down = total(at_position, square_along.astype(f32), 1)
    position_along = total(route_down == square_along.astype(f32), square_down.astype(f32), 0)
    first_row = (span_ref[0] * span_rows).astype(f32)

    def in_first(position):
        return (position >= first_row) & (position < first_row + span_rows)

    from_stale = jnp.where(in_first(position_down), 1.0, 0.0) * jnp.where(
        in_first(position_along), 0.0, 1.0
    )
    kind = jnp.where(req_down == req_along, 1.0 + from_stale, 0.0)
    stale_cols = stale_ref.shape[1]
    aux_ref[:, :stale_cols] = jnp.dot(
        jnp.where(at_position, 1.0, 0.0).astype(BF16),
        stale_ref[...],
        preferred_element_type=f32,
    ).astype(BF16)
    aux_ref[:, stale_cols:] = kind.astype(BF16)
    own = (down(own_rows, reqs) + req_ref[0] * own_rows).astype(f32)
    own_req = total(own >= starts_along, 1.0, 1) - 1.0
    for part in range(mod_ref.shape[0]):
        chosen = jnp.zeros(mod_ref.shape[1:], f32)
        for req in range(reqs):
            chosen = chosen + jnp.where(own_req == req, 1.0, 0.0) * modulation_ref[
                part, req : req + 1, :
            ]
        mod_ref[part] = chosen


def pack_kernel(qkv_ref, mlp_ref, attn_out_ref, mlp_out_ref, packed_ref, sems):
    width, qkv_cols = qkv_ref.shape
    head_dim, units = attn_out_ref.shape[0], mlp_out_ref.shape[0]
    cols = packed_ref.shape[1]
    moves = [
        (qkv_ref, packed_ref.at[pl.ds(0, width), pl.ds(0, qkv_cols)]),
        (mlp_ref, packed_ref.at[pl.ds(0, width), pl.ds(qkv_cols, units)]),
    ]
    for cut in range(width // cols):
        first = width + cut * (head_dim + units)
        span = pl.ds(cut * cols, cols)
        moves += [
            (attn_out_ref.at[:, span], packed_ref.at[pl.ds(first, head_dim), :]),
            (mlp_out_ref.at[:, span], packed_ref.at[pl.ds(first + head_dim, units), :]),
        ]
    copies = [
        pltpu.make_async_copy(source, target, sems.at[i])
        for i, (source, target) in enumerate(moves)
    ]
    for copy in copies:
        copy.start()
    for copy in copies:
        copy.wait()


def attend(qkv, aux_ref):
    head_dim = qkv.shape[1] // 3
    rows = qkv.shape[0]
    stale_cols = 2 * head_dim
    query = qkv[:, :head_dim]
    keys = jnp.concatenate([qkv[:, head_dim:stale_cols], aux_ref[:, :head_dim]], axis=0)
    values = jnp.concatenate([qkv[:, stale_cols:], aux_ref[:, head_dim:stale_cols]], axis=0)
    kind = aux_ref[:, stale_cols:].astype(jnp.float32)
    from_stale = kind > 1.5
    both = lax.dot_general(
        query, keys, (((1,), (1,)), ((), ())), preferred_element_type=jnp.float32
    )
    scores = jnp.where(from_stale, both[:, rows:], both[:, :rows]) / jnp.sqrt(
        jnp.float32(head_dim)
    )
    scores = jnp.where(kind > 0.5, scores, -jnp.inf)
    exps = jnp.exp(scores - jnp.max(scores, axis=-1, keepdims=True))
    weights = jnp.concatenate(
        [jnp.where(from_stale, 0.0, exps), jnp.where(from_stale, exps, 0.0)], axis=1
    ).astype(BF16)
    attended = jnp.dot(weights, values, preferred_element_type=jnp.float32)
    return (attended / jnp.sum(exps, axis=-1, keepdims=True)).astype(BF16)


def block_kernel(
    rows_ref,
    qkv_ref,
    mlp_ref,
    attn_out_ref,
    mlp_out_ref,
    aux_ref,
    out_ref,
):
    qkv = jnp.dot(rows_ref[...], qkv_ref[...], preferred_element_type=jnp.float32).astype(BF16)
    attended = attend(qkv, aux_ref)
    mlp_act = gelu_tanh(
        jnp.dot(rows_ref[...], mlp_ref[...], preferred_element_type=jnp.float32)
    ).astype(BF16)
    cols = out_ref.shape[1] // WIDTH_CUTS
    for cut in range(WIDTH_CUTS):
        span = slice(cut * cols, (cut + 1) * cols)
        out_ref[:, span] = (
            jnp.dot(attended, attn_out_ref[:, span], preferred_element_type=jnp.float32)
            + jnp.dot(mlp_act, mlp_out_ref[:, span], preferred_element_type=jnp.float32)
        ).astype(BF16)


def packed_block_kernel(qkv_cols, rows_ref, packed_ref, aux_ref, out_ref):
    width = rows_ref.shape[1]
    cols = packed_ref.shape[1]
    cuts = width // cols
    depth = (packed_ref.shape[0] - width) // cuts
    total = jnp.dot(
        rows_ref[...], packed_ref[:width, :], preferred_element_type=jnp.float32
    )
    attended = attend(total[:, :qkv_cols].astype(BF16), aux_ref)
    mlp_act = gelu_tanh(total[:, qkv_cols:]).astype(BF16)
    inner = jnp.concatenate([attended, mlp_act], axis=1)
    for cut in range(cuts):
        first = width + cut * depth
        out_ref[:, cut * cols : (cut + 1) * cols] = jnp.dot(
            inner, packed_ref[first : first + depth, :], preferred_element_type=jnp.float32
        ).astype(BF16)


def spread_normed(current, mod_ref, out_ref):
    row_mean = jnp.mean(current, axis=-1, keepdims=True)
    centered = current - row_mean
    row_var = jnp.mean(centered * centered, axis=-1, keepdims=True)
    normed = centered * lax.rsqrt(row_var + 1e-06) * (1.0 + mod_ref[1]) + mod_ref[0]
    twice = jnp.concatenate([normed, normed], axis=0).astype(BF16)
    for first in range(0, out_ref.shape[0], TILE):
        out_ref[first : first + TILE, :] = twice


def summed(shares_ref, current_ref, mod_ref):
    branch = shares_ref[:TILE, :].astype(jnp.float32)
    for first in range(TILE, shares_ref.shape[0], TILE):
        branch = branch + shares_ref[first : first + TILE, :].astype(jnp.float32)
    branch = branch[: TILE // 2] + branch[TILE // 2 :]
    return (current_ref[...].astype(jnp.float32) + mod_ref[2] * branch).astype(BF16)


def nothing_kernel(*refs):
    pass


def keep_kernel(section_ref, aux_hbm, mod_hbm, aux_ref, mod_ref, sems):
    @pl.when(section_ref[0] >= 2)
    def _():
        copies = [
            pltpu.make_async_copy(aux_hbm, aux_ref, sems.at[0]),
            pltpu.make_async_copy(mod_hbm, mod_ref, sems.at[1]),
        ]
        for copy in copies:
            copy.start()
        for copy in copies:
            copy.wait()


def norm_kernel(current_ref, mod_ref, *refs):
    spread_normed(current_ref[...].astype(jnp.float32), mod_ref, refs[-1])


def sum_kernel(shares_ref, current_ref, mod_ref, out_ref):
    out_ref[...] = summed(shares_ref, current_ref, mod_ref)


def shards(
    latents,
    patch_route,
    request_len,
    span_order,
    modulation,
    w_qkv,
    w_mlp_in,
    w_out_attn,
    w_out_mlp,
    stale_kv,
):
    section_count = lax.axis_size("section")
    req_count = lax.axis_size("req")
    section_index = lax.axis_index("section")
    req_index = lax.axis_index("req")
    patches = patch_route.shape[0]
    own_rows, width = latents.shape
    qkv_cols = w_qkv.shape[3]
    head_dim = w_out_attn.shape[2]
    units = w_mlp_in.shape[2]

    near = pl.BlockSpec(memory_space=pltpu.SMEM)
    operands = (
        span_order,
        patch_route.reshape(1, patches),
        request_len.reshape(1, -1),
        modulation[0].swapaxes(0, 1),
        stale_kv[0, :, 0],
    )
    aux, mod = pl.pallas_call(
        prepare_kernel,
        out_shape=(
            pltpu.VMEM((patches, 2 * head_dim + patches), BF16),
            pltpu.VMEM((3, own_rows, width), jnp.float32),
        ),
        in_specs=[near] + [ANY] * 5,
        out_specs=(VMEM, VMEM),
        scratch_shapes=[pltpu.SMEM(span_order.shape, span_order.dtype)]
        + [pltpu.VMEM(value.shape, value.dtype) for value in operands[1:]]
        + [pltpu.SemaphoreType.DMA((5,))],
        compiler_params=LARGE,
        name="prepare",
    )(req_index.astype(jnp.int32).reshape(1), *operands)
    mod, aux = lax.optimization_barrier((mod, aux))
    own_weights = (w_qkv[0, :, 0], w_mlp_in[0], w_out_attn[0, 0], w_out_mlp[0])
    to_sibling = [
        (i, i + req_count)
        for i in range(2 * req_count, section_count * req_count)
        if i // req_count % 2 == 0
    ]
    packed_cols = qkv_cols + units
    pack = pl.pallas_call(
        pack_kernel,
        out_shape=jax.ShapeDtypeStruct(
            (width + width // packed_cols * (head_dim + units), packed_cols), BF16
        ),
        in_specs=[ANY] * 4,
        out_specs=VMEM,
        compiler_params=PARAMS,
        scratch_shapes=[pltpu.SemaphoreType.DMA((2 + 2 * (width // packed_cols),))],
        name="pack_weights",
    )

    def chip_sections(weights, aux, mod):
        own = (pack(*weights), aux, mod)
        return own[0], *(lax.ppermute(value, AXES, to_sibling) for value in own)

    def unused(function):
        def nothing(*values):
            shapes, tree = jax.tree.flatten(jax.eval_shape(function, *values))
            results = pl.pallas_call(
                nothing_kernel,
                out_shape=tuple(jax.ShapeDtypeStruct(v.shape, v.dtype) for v in shapes),
                out_specs=(ANY,) * len(shapes),
                name="unused",
            )()
            return jax.tree.unflatten(tree, results)

        return nothing

    all_rows = jax.ShapeDtypeStruct((patches, width), BF16)
    own = jax.ShapeDtypeStruct((own_rows, width), BF16)
    def norm(current, mod, *weights):
        return pl.pallas_call(
            norm_kernel,
            out_shape=all_rows,
            in_specs=[VMEM] * 2 + [ANY] * len(weights),
            out_specs=VMEM,
            compiler_params=PARAMS,
            name="spread_normed",
        )(current, mod, *weights)

    def heads_and_units(everyone, weights, aux):
        kernel = block_kernel
        if len(weights) == 1:
            kernel = functools.partial(packed_block_kernel, qkv_cols)
        return pl.pallas_call(
            kernel,
            out_shape=all_rows,
            in_specs=[VMEM] * (2 + len(weights)),
            out_specs=VMEM,
            compiler_params=PARAMS,
            name="heads_and_units",
        )(
            everyone,
            *[pltpu.with_memory_space_constraint(value, pltpu.VMEM) for value in weights],
            aux,
        )

    add_shares = pl.pallas_call(
        sum_kernel,
        out_shape=own,
        in_specs=[VMEM] * 3,
        out_specs=VMEM,
        compiler_params=PARAMS,
        name="add_shares",
    )

    def exchange(value):
        value = value.reshape(req_count, own_rows, width)
        value = lax.all_to_all(value, "req", split_axis=0, concat_axis=0, tiled=True)
        return value.reshape(patches, width)

    def one_section(current, *section):
        *weights, aux, mod = section
        everyone = exchange(norm(current, mod, *weights, aux))
        partial_value = heads_and_units(everyone, weights, aux)
        return add_shares(exchange(partial_value), current, mod)

    def when(section, current, held):
        return lax.cond(
            section_index == section, one_section, unused(one_section), current, *held
        )

    def hand_over(current, sections):
        pairs = [(a * req_count + i, b * req_count + i) for a, b in sections for i in range(req_count)]
        return lax.ppermute(current, AXES, pairs)

    def chip_turn(chip, current):
        current = when(2 * chip + 1, current, first_held)
        return when(2 * chip + 1, current, second_held)

    start = (*own_weights, aux, mod)
    current = lax.fori_loop(
        0, 2, lambda section, rows: hand_over(when(section, rows, start), [(0, 1), (1, 3)]), latents
    )
    own_packed, *first_held = lax.cond(
        section_index >= 2, chip_sections, unused(chip_sections), own_weights, aux, mod
    )
    own_packed, first_packed = pl.pallas_call(
        nothing_kernel,
        out_shape=(jax.ShapeDtypeStruct(own_packed.shape, BF16),) * 2,
        in_specs=[ANY] * 2,
        out_specs=(ANY,) * 2,
        input_output_aliases={0: 0, 1: 1},
        name="pass_on",
    )(own_packed, first_held[0])
    small = pl.pallas_call(
        keep_kernel,
        out_shape=tuple(pltpu.VMEM(value.shape, value.dtype) for value in (aux, mod)),
        in_specs=[near] + [ANY] * 2,
        out_specs=(VMEM, VMEM),
        scratch_shapes=[pltpu.SemaphoreType.DMA((2,))],
        compiler_params=LARGE,
        name="keep",
    )(section_index.astype(jnp.int32).reshape(1), *first_held[1:])
    first_held = (first_packed, *small)
    second_held = (own_packed, aux, mod)
    last = section_count // 2 - 1
    onward = [[(2 * c + 1, 2 * c + 3) for c in range(first, last, 2)] for first in (1, 2)]

    def two_chips(turn, current):
        for i, pairs in enumerate(onward):
            current = hand_over(chip_turn(2 * turn + 1 + i, current), pairs)
        return current

    current = lax.fori_loop(0, last // 2, two_chips, current)
    current = chip_turn(last, current)
    pieces = current.reshape(own_rows, section_count, width // section_count).swapaxes(0, 1)
    pieces = lax.all_to_all(pieces, "section", split_axis=0, concat_axis=0, tiled=True)
    return pieces[section_count - 1]


def solution(mesh):
    in_specs = (
        P("req", None),
        P(),
        P(),
        P(),
        P("section", None, None, None),
        P("section", None, "req", None),
        P("section", None, "req"),
        P("section", "req", None, None),
        P("section", "req", None),
        P("section", None, "req", None),
    )
    out_specs = P("req", "section")
    return jax.shard_map(shards, mesh=mesh, in_specs=in_specs, out_specs=out_specs, check_vma=False)
```

```python
import functools

import jax
import jax.numpy as jnp
from jax import lax
from jax.experimental import pallas as pl
from jax.experimental.pallas import tpu as pltpu
from jax.sharding import PartitionSpec as P

AXES = ("section", "req")
BF16 = jnp.bfloat16
WIDTH_CUTS = 4
TILE = 16
HELD = 10
LANES = 128
SECOND = 48
VMEM = pl.BlockSpec(memory_space=pltpu.VMEM)
ANY = pl.BlockSpec(memory_space=pl.ANY)
LARGE = pltpu.CompilerParams(vmem_limit_bytes=58 * 1024 * 1024)
PARAMS = pltpu.CompilerParams(vmem_limit_bytes=16 * 1024 * 1024)


def gelu_tanh(values):
    return (
        0.5
        * values
        * (1.0 + jnp.tanh(0.7978845608028654 * (values + 0.044715 * values * values * values)))
    )


def down(rows, cols):
    return lax.broadcasted_iota(jnp.int32, (rows, cols), 0)


def along(rows, cols):
    return lax.broadcasted_iota(jnp.int32, (rows, cols), 1)


def total(mask, values, axis):
    return jnp.sum(jnp.where(mask, values, 0.0), axis=axis, keepdims=True)


def request_starts(len_ref):
    reqs = len_ref.shape[1]
    lens = jnp.broadcast_to(len_ref[...].astype(jnp.float32), (reqs, reqs))
    lens_down = total(down(reqs, reqs) == along(reqs, reqs), lens, 1)
    return (
        total(down(reqs, reqs) < along(reqs, reqs), lens_down, 0),
        total(along(reqs, reqs) < down(reqs, reqs), lens, 1),
    )


def write_aux(aux_ref, row_of, span_ref, route_ref, len_ref, stale_ref):
    patches, reqs = route_ref.shape[1], len_ref.shape[1]
    rows, stale_cols = aux_ref.shape[0], stale_ref.shape[1]
    places = aux_ref.shape[1] - stale_cols
    span_rows = patches // span_ref.shape[0]
    f32 = jnp.float32
    starts_along, starts_down = request_starts(len_ref)
    row_down = row_of(down(rows, reqs)).astype(f32)
    row_along = row_of(along(reqs, places)).astype(f32)
    req_down = total(row_down >= starts_along, 1.0, 1) - 1.0
    req_along = total(row_along >= starts_down, 1.0, 0) - 1.0
    route = jnp.broadcast_to(route_ref[...], (patches, patches))
    route_down = total(down(patches, patches) == along(patches, patches), route.astype(f32), 1)
    at_position = row_of(down(rows, patches)) == jnp.broadcast_to(
        route_ref[...], (rows, patches)
    )
    position_down = total(at_position, along(rows, patches).astype(f32), 1)
    position_along = total(
        route_down == row_of(along(patches, places)).astype(f32),
        down(patches, places).astype(f32),
        0,
    )
    first_row = (span_ref[0] * span_rows).astype(f32)

    def in_first(position):
        return (position >= first_row) & (position < first_row + span_rows)

    from_stale = jnp.where(in_first(position_down), 1.0, 0.0) * jnp.where(
        in_first(position_along), 0.0, 1.0
    )
    counts = jnp.where(along(rows, places) < rows, 1.0, 0.0)
    kind = jnp.where(req_down == req_along, (1.0 + from_stale) * counts, 0.0)
    aux_ref[:, :stale_cols] = jnp.dot(
        jnp.where(at_position, 1.0, 0.0).astype(BF16),
        stale_ref[...],
        preferred_element_type=f32,
    ).astype(BF16)
    aux_ref[:, stale_cols:] = kind.astype(BF16)


def fetch(pairs, sems):
    copies = [
        pltpu.make_async_copy(source, target, sems.at[i])
        for i, (source, target) in enumerate(pairs)
    ]
    for copy in copies:
        copy.start()
    for copy in copies:
        copy.wait()


def prepare_kernel(
    req_ref,
    span_hbm,
    route_hbm,
    len_hbm,
    modulation_hbm,
    stale_hbm,
    aux_ref,
    mod_ref,
    span_ref,
    route_ref,
    len_ref,
    modulation_ref,
    stale_ref,
    sems,
):
    fetch(
        (
            (span_hbm, span_ref),
            (route_hbm, route_ref),
            (len_hbm, len_ref),
            (modulation_hbm, modulation_ref),
            (stale_hbm, stale_ref),
        ),
        sems,
    )
    write_aux(aux_ref, lambda place: place, span_ref, route_ref, len_ref, stale_ref)
    reqs, own_rows = len_ref.shape[1], mod_ref.shape[1]
    own = (down(own_rows, reqs) + req_ref[0] * own_rows).astype(jnp.float32)
    own_req = total(own >= request_starts(len_ref)[0], 1.0, 1) - 1.0
    for part in range(mod_ref.shape[0]):
        chosen = jnp.zeros(mod_ref.shape[1:], jnp.float32)
        for req in range(reqs):
            chosen = chosen + jnp.where(own_req == req, 1.0, 0.0) * modulation_ref[
                part, req : req + 1, :
            ]
        mod_ref[part] = chosen


def fold(rows):
    cols = rows[0].shape[1] // 8
    return jnp.concatenate(
        [
            jnp.concatenate([row[:, s * cols : (s + 1) * cols] for s in range(8)], axis=0)
            for row in rows
        ],
        axis=1,
    )


def prepare_half_kernel(
    req_ref,
    span_hbm,
    route_hbm,
    len_hbm,
    modulation_hbm,
    stale_hbm,
    mine_ref,
    theirs_ref,
    mod_ref,
    span_ref,
    route_ref,
    len_ref,
    modulation_ref,
    stale_ref,
    sems,
):
    fetch(
        (
            (span_hbm, span_ref),
            (route_hbm, route_ref),
            (len_hbm, len_ref),
            (modulation_hbm, modulation_ref),
            (stale_hbm, stale_ref),
        ),
        sems,
    )
    base = jnp.where(req_ref[0] >= 8, SECOND, 0)
    seat = jnp.bitwise_and(req_ref[0], 7)
    for first, aux_ref in ((base, mine_ref), (SECOND - base, theirs_ref)):

        def row_of(place):
            return first + jnp.bitwise_and(place, 7) * HELD + lax.shift_right_logical(place, 3)

        write_aux(aux_ref, row_of, span_ref, route_ref, len_ref, stale_ref)
    reqs = len_ref.shape[1]
    held = (down(16, reqs) + base + seat * HELD).astype(jnp.float32)
    held_req = total(held >= request_starts(len_ref)[0], 1.0, 1) - 1.0
    for part in range(mod_ref.shape[0]):
        chosen = jnp.zeros((16, modulation_ref.shape[2]), jnp.float32)
        for req in range(reqs):
            chosen = chosen + jnp.where(held_req == req, 1.0, 0.0) * modulation_ref[
                part, req : req + 1, :
            ]
        mod_ref[part] = fold([chosen[i : i + 1] for i in range(HELD)])


def same_kernel(values_ref, out_ref):
    out_ref[...] = values_ref[...]


def fold_kernel(req_ref, first_ref, second_ref, out_ref):
    skipped = jnp.bitwise_and(jnp.bitwise_and(req_ref[0], 7) * HELD, 7)
    rows = jnp.concatenate(
        [first_ref[...].astype(jnp.float32), second_ref[...].astype(jnp.float32)], axis=0
    ).astype(BF16)
    pick = jnp.where(along(16, 16) == down(16, 16) + skipped, 1.0, 0.0).astype(BF16)
    picked = jnp.dot(pick, rows, preferred_element_type=jnp.float32)
    out_ref[...] = fold([picked[i : i + 1] for i in range(HELD)]).astype(BF16)


def unfold_kernel(current_ref, out_ref):
    cols = current_ref.shape[1] // HELD
    current = current_ref[...].astype(jnp.float32)
    rows = [
        jnp.concatenate(
            [current[s : s + 1, i * cols : (i + 1) * cols] for s in range(8)], axis=1
        )
        for i in range(HELD)
    ]
    rows.append(jnp.zeros((out_ref.shape[0] - HELD, 8 * cols), jnp.float32))
    out_ref[...] = jnp.concatenate(rows, axis=0).astype(BF16)


def place_kernel(req_ref, rows_ref, len_ref, out_ref):
    patches, held = out_ref.shape[0], rows_ref.shape[0]
    base = jnp.where(req_ref[0] >= 8, SECOND, 0)
    held_first = base + jnp.bitwise_and(req_ref[0], 7) * HELD
    starts, _ = request_starts(len_ref)
    ends = starts + len_ref[...].astype(jnp.float32)
    border = jnp.max(jnp.where(ends <= 8 * HELD, ends, 0.0), axis=1, keepdims=True)
    place = down(patches, held)
    before = place.astype(jnp.float32) < border
    first_half = jnp.where(base == 0, 1.0, 0.0)
    counts = jnp.where(before, first_half, 1.0 - first_half)
    here = jnp.where(
        (place == held_first + along(patches, held)) & (along(patches, held) < HELD), counts, 0.0
    )
    out_ref[...] = jnp.dot(
        here.astype(BF16), rows_ref[...], preferred_element_type=jnp.float32
    ).astype(BF16)


def pack_kernel(qkv_ref, mlp_ref, attn_out_ref, mlp_out_ref, packed_ref, sems):
    width, qkv_cols = qkv_ref.shape
    head_dim, units = attn_out_ref.shape[0], mlp_out_ref.shape[0]
    cols = packed_ref.shape[1]
    moves = [
        (qkv_ref, packed_ref.at[pl.ds(0, width), pl.ds(0, qkv_cols)]),
        (mlp_ref, packed_ref.at[pl.ds(0, width), pl.ds(qkv_cols, units)]),
    ]
    for cut in range(width // cols):
        first = width + cut * (head_dim + units)
        span = pl.ds(cut * cols, cols)
        moves += [
            (attn_out_ref.at[:, span], packed_ref.at[pl.ds(first, head_dim), :]),
            (mlp_out_ref.at[:, span], packed_ref.at[pl.ds(first + head_dim, units), :]),
        ]
    copies = [
        pltpu.make_async_copy(source, target, sems.at[i])
        for i, (source, target) in enumerate(moves)
    ]
    for copy in copies:
        copy.start()
    for copy in copies:
        copy.wait()


def attend(qkv, aux_ref):
    head_dim = qkv.shape[1] // 3
    rows = qkv.shape[0]
    stale_cols = 2 * head_dim
    places = aux_ref.shape[1] - stale_cols

    def both_kinds(fresh, stale):
        if rows == places:
            return jnp.concatenate([fresh, stale], axis=0)
        none = jnp.zeros((places - rows, head_dim), BF16)
        return jnp.concatenate([fresh, none, stale, none], axis=0)

    query = qkv[:, :head_dim]
    keys = both_kinds(qkv[:, head_dim:stale_cols], aux_ref[:, :head_dim])
    values = both_kinds(qkv[:, stale_cols:], aux_ref[:, head_dim:stale_cols])
    kind = aux_ref[:, stale_cols:].astype(jnp.float32)
    from_stale = kind > 1.5
    both = lax.dot_general(
        query, keys, (((1,), (1,)), ((), ())), preferred_element_type=jnp.float32
    )
    scores = jnp.where(from_stale, both[:, places:], both[:, :places]) / jnp.sqrt(
        jnp.float32(head_dim)
    )
    scores = jnp.where(kind > 0.5, scores, -jnp.inf)
    exps = jnp.exp(scores - jnp.max(scores, axis=-1, keepdims=True))
    weights = jnp.concatenate(
        [jnp.where(from_stale, 0.0, exps), jnp.where(from_stale, exps, 0.0)], axis=1
    ).astype(BF16)
    attended = jnp.dot(weights, values, preferred_element_type=jnp.float32)
    return (attended / jnp.sum(exps, axis=-1, keepdims=True)).astype(BF16)


def block_kernel(
    rows_ref,
    qkv_ref,
    mlp_ref,
    attn_out_ref,
    mlp_out_ref,
    aux_ref,
    out_ref,
):
    qkv = jnp.dot(rows_ref[...], qkv_ref[...], preferred_element_type=jnp.float32).astype(BF16)
    attended = attend(qkv, aux_ref)
    mlp_act = gelu_tanh(
        jnp.dot(rows_ref[...], mlp_ref[...], preferred_element_type=jnp.float32)
    ).astype(BF16)
    cols = out_ref.shape[1] // WIDTH_CUTS
    for cut in range(WIDTH_CUTS):
        span = slice(cut * cols, (cut + 1) * cols)
        out_ref[:, span] = (
            jnp.dot(attended, attn_out_ref[:, span], preferred_element_type=jnp.float32)
            + jnp.dot(mlp_act, mlp_out_ref[:, span], preferred_element_type=jnp.float32)
        ).astype(BF16)


def packed_block_kernel(qkv_cols, rows_ref, packed_ref, aux_ref, out_ref):
    width = rows_ref.shape[1]
    cols = packed_ref.shape[1]
    cuts = width // cols
    depth = (packed_ref.shape[0] - width) // cuts
    total = jnp.dot(
        rows_ref[...], packed_ref[:width, :], preferred_element_type=jnp.float32
    )
    attended = attend(total[:, :qkv_cols].astype(BF16), aux_ref)
    mlp_act = gelu_tanh(total[:, qkv_cols:]).astype(BF16)
    inner = jnp.concatenate([attended, mlp_act], axis=1)
    for cut in range(cuts):
        first = width + cut * depth
        out_ref[:, cut * cols : (cut + 1) * cols] = jnp.dot(
            inner, packed_ref[first : first + depth, :], preferred_element_type=jnp.float32
        ).astype(BF16)


def half_block_kernel(
    qkv_cols,
    rows_ref,
    packed_ref,
    their_packed_hbm,
    aux_ref,
    their_aux_ref,
    out_ref,
    their_packed_ref,
    spread_ref,
    inputs_ref,
    sems,
):
    width = inputs_ref.shape[1]
    rest = packed_ref.shape[0] - width
    reads = [
        pltpu.make_async_copy(
            their_packed_hbm.at[pl.ds(first, count), :],
            their_packed_ref.at[pl.ds(first, count), :],
            sems.at[i],
        )
        for i, (first, count) in enumerate(((0, width), (width, rest)))
    ]
    for read in reads:
        read.start()
    piece = width // 8
    cols = packed_ref.shape[1]
    cuts = width // cols
    depth = (packed_ref.shape[0] - width) // cuts
    tiles = piece // LANES
    for tile in range(spread_ref.shape[0]):
        spread_ref[tile] = rows_ref[:, tile * LANES : (tile + 1) * LANES].astype(jnp.float32)
    for i in range(0, HELD, 2):
        for s in range(8):
            for t in range(tiles):
                inputs_ref[
                    8 * i : 8 * i + 16, s * piece + t * LANES : s * piece + (t + 1) * LANES
                ] = jnp.concatenate(
                    [spread_ref[k * tiles + t, pl.ds(s, 8, stride=8), :] for k in (i, i + 1)],
                    axis=0,
                ).astype(BF16)
    sums = [
        jnp.dot(inputs_ref[...], packed_ref[:width, :], preferred_element_type=jnp.float32)
    ]
    reads[0].wait()
    sums.append(
        jnp.dot(inputs_ref[...], their_packed_ref[:width, :], preferred_element_type=jnp.float32)
    )
    inner = []
    for values, extra in zip(sums, (aux_ref, their_aux_ref)):
        attended = attend(values[:, :qkv_cols].astype(BF16), extra)
        mlp_act = gelu_tanh(values[:, qkv_cols:]).astype(BF16)
        inner.append(jnp.concatenate([attended, mlp_act], axis=1))
    reads[1].wait()
    for cut in range(cuts):
        first = width + cut * depth
        out = jnp.dot(
            inner[0], packed_ref[first : first + depth, :], preferred_element_type=jnp.float32
        ) + jnp.dot(
            inner[1],
            their_packed_ref[first : first + depth, :],
            preferred_element_type=jnp.float32,
        )
        for k in range(cols // piece):
            s = cut * (cols // piece) + k
            for i in range(HELD):
                for t in range(tiles):
                    first = k * piece + t * LANES
                    spread_ref[i * tiles + t, pl.ds(s, 8, stride=8), :] = out[
                        8 * i : 8 * i + 8, first : first + LANES
                    ]
    for tile in range(spread_ref.shape[0]):
        out_ref[:, tile * LANES : (tile + 1) * LANES] = spread_ref[tile].astype(BF16)


def of_row(values):
    return jnp.sum(jnp.sum(values, axis=1, keepdims=True), axis=0, keepdims=True)


def half_norm_kernel(current_ref, mod_ref, *refs):
    out_ref = refs[-1]
    current = current_ref[...].astype(jnp.float32)
    cols = current.shape[1] // HELD
    normed = []
    for i in range(HELD):
        values = current[:, i * cols : (i + 1) * cols]
        centered = values - of_row(values) / (8 * cols)
        normed.append(centered * lax.rsqrt(of_row(centered * centered) / (8 * cols) + 1e-06))
    normed = jnp.concatenate(normed, axis=1) * (1.0 + mod_ref[1]) + mod_ref[0]
    twice = jnp.concatenate([normed, normed], axis=0).astype(BF16)
    for first in range(0, out_ref.shape[0], TILE):
        out_ref[first : first + TILE, :] = twice


def spread_normed(current, mod_ref, out_ref):
    row_mean = jnp.mean(current, axis=-1, keepdims=True)
    centered = current - row_mean
    row_var = jnp.mean(centered * centered, axis=-1, keepdims=True)
    normed = centered * lax.rsqrt(row_var + 1e-06) * (1.0 + mod_ref[1]) + mod_ref[0]
    twice = jnp.concatenate([normed, normed], axis=0).astype(BF16)
    for first in range(0, out_ref.shape[0], TILE):
        out_ref[first : first + TILE, :] = twice


def summed(shares_ref, current_ref, mod_ref):
    branch = shares_ref[:TILE, :].astype(jnp.float32)
    for first in range(TILE, shares_ref.shape[0], TILE):
        branch = branch + shares_ref[first : first + TILE, :].astype(jnp.float32)
    branch = branch[: TILE // 2] + branch[TILE // 2 :]
    return (current_ref[...].astype(jnp.float32) + mod_ref[2] * branch).astype(BF16)


def nothing_kernel(*refs):
    pass


def keep_kernel(least, section_ref, *refs):
    *refs, sems = refs
    count = len(refs) // 2

    @pl.when(section_ref[0] >= least)
    def _():
        fetch(list(zip(refs[:count], refs[count:])), sems)


def norm_kernel(current_ref, mod_ref, *refs):
    spread_normed(current_ref[...].astype(jnp.float32), mod_ref, refs[-1])


def sum_kernel(shares_ref, current_ref, mod_ref, out_ref):
    out_ref[...] = summed(shares_ref, current_ref, mod_ref)


def shards(
    latents,
    patch_route,
    request_len,
    span_order,
    modulation,
    w_qkv,
    w_mlp_in,
    w_out_attn,
    w_out_mlp,
    stale_kv,
):
    section_count = lax.axis_size("section")
    req_count = lax.axis_size("req")
    section_index = lax.axis_index("section")
    req_index = lax.axis_index("req")
    patches = patch_route.shape[0]
    own_rows, width = latents.shape
    qkv_cols = w_qkv.shape[3]
    head_dim = w_out_attn.shape[2]
    units = w_mlp_in.shape[2]

    near = pl.BlockSpec(memory_space=pltpu.SMEM)
    operands = (
        span_order,
        patch_route.reshape(1, patches),
        request_len.reshape(1, -1),
        modulation[0].swapaxes(0, 1),
        stale_kv[0, :, 0],
    )
    aux, mod = pl.pallas_call(
        prepare_kernel,
        out_shape=(
            pltpu.VMEM((patches, 2 * head_dim + patches), BF16),
            pltpu.VMEM((3, own_rows, width), jnp.float32),
        ),
        in_specs=[near] + [ANY] * 5,
        out_specs=(VMEM, VMEM),
        scratch_shapes=[pltpu.SMEM(span_order.shape, span_order.dtype)]
        + [pltpu.VMEM(value.shape, value.dtype) for value in operands[1:]]
        + [pltpu.SemaphoreType.DMA((5,))],
        compiler_params=LARGE,
        name="prepare",
    )(req_index.astype(jnp.int32).reshape(1), *operands)
    mod, aux = lax.optimization_barrier((mod, aux))
    own_weights = (w_qkv[0, :, 0], w_mlp_in[0], w_out_attn[0, 0], w_out_mlp[0])
    to_sibling = [
        (i, i + req_count)
        for i in range(2 * req_count, section_count * req_count)
        if i // req_count % 2 == 0
    ]
    packed_cols = qkv_cols + units
    pack = pl.pallas_call(
        pack_kernel,
        out_shape=jax.ShapeDtypeStruct(
            (width + width // packed_cols * (head_dim + units), packed_cols), BF16
        ),
        in_specs=[ANY] * 4,
        out_specs=VMEM,
        compiler_params=PARAMS,
        scratch_shapes=[pltpu.SemaphoreType.DMA((2 + 2 * (width // packed_cols),))],
        name="pack_weights",
    )

    def chip_sections(weights, aux, mod):
        own = (pack(*weights), aux, mod)
        return own[0], *(lax.ppermute(value, AXES, to_sibling) for value in own)

    def unused(function):
        def nothing(*values):
            shapes, tree = jax.tree.flatten(jax.eval_shape(function, *values))
            results = pl.pallas_call(
                nothing_kernel,
                out_shape=tuple(jax.ShapeDtypeStruct(v.shape, v.dtype) for v in shapes),
                out_specs=(ANY,) * len(shapes),
                name="unused",
            )()
            return jax.tree.unflatten(tree, results)

        return nothing

    all_rows = jax.ShapeDtypeStruct((patches, width), BF16)
    own = jax.ShapeDtypeStruct((own_rows, width), BF16)
    def norm(current, mod, *weights):
        return pl.pallas_call(
            norm_kernel,
            out_shape=all_rows,
            in_specs=[VMEM] * 2 + [ANY] * len(weights),
            out_specs=VMEM,
            compiler_params=PARAMS,
            name="spread_normed",
        )(current, mod, *weights)

    def heads_and_units(everyone, weights, aux):
        kernel = block_kernel
        if len(weights) == 1:
            kernel = functools.partial(packed_block_kernel, qkv_cols)
        return pl.pallas_call(
            kernel,
            out_shape=all_rows,
            in_specs=[VMEM] * (2 + len(weights)),
            out_specs=VMEM,
            compiler_params=PARAMS,
            name="heads_and_units",
        )(
            everyone,
            *[pltpu.with_memory_space_constraint(value, pltpu.VMEM) for value in weights],
            aux,
        )

    add_shares = pl.pallas_call(
        sum_kernel,
        out_shape=own,
        in_specs=[VMEM] * 3,
        out_specs=VMEM,
        compiler_params=PARAMS,
        name="add_shares",
    )

    def exchange(value):
        value = value.reshape(req_count, own_rows, width)
        value = lax.all_to_all(value, "req", split_axis=0, concat_axis=0, tiled=True)
        return value.reshape(patches, width)

    def one_section(current, *section):
        *weights, aux, mod = section
        everyone = exchange(norm(current, mod, *weights, aux))
        partial_value = heads_and_units(everyone, weights, aux)
        return add_shares(exchange(partial_value), current, mod)

    def when(section, current, held):
        return lax.cond(
            section_index == section, one_section, unused(one_section), current, *held
        )

    def hand_over(current, sections):
        pairs = [(a * req_count + i, b * req_count + i) for a, b in sections for i in range(req_count)]
        return lax.ppermute(current, AXES, pairs)

    start = (*own_weights, aux, mod)
    current = hand_over(when(0, latents, start), [(0, 1)])
    current = hand_over(when(1, current, start), [(1, 3)])

    def settle(least, packed, small):
        packed = pl.pallas_call(
            nothing_kernel,
            out_shape=tuple(jax.ShapeDtypeStruct(value.shape, BF16) for value in packed),
            in_specs=[ANY] * len(packed),
            out_specs=(ANY,) * len(packed),
            input_output_aliases={i: i for i in range(len(packed))},
            name="pass_on",
        )(*packed)
        small = pl.pallas_call(
            functools.partial(keep_kernel, least),
            out_shape=tuple(pltpu.VMEM(value.shape, value.dtype) for value in small),
            in_specs=[near] + [ANY] * len(small),
            out_specs=(VMEM,) * len(small),
            scratch_shapes=[pltpu.SemaphoreType.DMA((len(small),))],
            compiler_params=LARGE,
            name="keep",
        )(section_index.astype(jnp.int32).reshape(1), *small)
        return packed, small

    own_packed, *first = lax.cond(
        section_index >= 2, chip_sections, unused(chip_sections), own_weights, aux, mod
    )
    (own_packed, first_packed), small = settle(2, (own_packed, first[0]), first[1:])
    first_held, own_held = (first_packed, *small), (own_packed, aux, mod)

    early = section_count // 4
    req_id = req_index.astype(jnp.int32).reshape(1)
    side = 4
    partner = [(side - 1 - r // side) * side + r % side for r in range(req_count)]
    window = (8 * HELD, 2 * head_dim + patches)
    folded = (8, HELD * width // 8)

    def late_sections(own_packed, first_packed, *operands):
        mine, theirs, mods = pl.pallas_call(
            prepare_half_kernel,
            out_shape=(
                jax.ShapeDtypeStruct(window, BF16),
                jax.ShapeDtypeStruct(window, BF16),
                jax.ShapeDtypeStruct((3, *folded), jnp.float32),
            ),
            in_specs=[near] + [ANY] * 5,
            out_specs=(VMEM,) * 3,
            scratch_shapes=[pltpu.SMEM(span_order.shape, span_order.dtype)]
            + [pltpu.VMEM(value.shape, value.dtype) for value in operands[1:]]
            + [pltpu.SemaphoreType.DMA((5,))],
            compiler_params=PARAMS,
            name="prepare_half",
        )(req_id, *operands)
        own = (mine, theirs, mods)
        pairs = [
            (i, i + req_count)
            for i in range(2 * early * req_count, section_count * req_count)
            if i // req_count % 2 == 0
        ]
        first = tuple(lax.ppermute(value, AXES, pairs) for value in own)
        swap = [
            (s * req_count + r, s * req_count + partner[r])
            for s in range(2 * early + 1, section_count, 2)
            for r in range(req_count)
        ]
        swapped = tuple(
            lax.ppermute(value, AXES, swap)
            for value in (first[1], own[1], first_packed, own_packed)
        )
        return (*swapped[2:], first[0], swapped[0], first[2], own[0], swapped[1], own[2])

    late = lax.cond(
        section_index >= 2 * early,
        late_sections,
        unused(late_sections),
        own_packed,
        first_packed,
        *operands,
    )
    their_packed, small = settle(2 * early, late[:2], late[2:])
    first_half = (first_packed, their_packed[0], *small[:3])
    own_half = (own_packed, their_packed[1], *small[3:])

    def half_step(current, packed, their_packed, aux, their_aux, mod):
        rows = jax.ShapeDtypeStruct((8 * 8, folded[1]), BF16)
        halves = [list(range(8)), list(range(8, 16))]

        def exchange(value):
            value = value.reshape(8, *folded)
            value = lax.all_to_all(
                value, "req", split_axis=0, concat_axis=0, tiled=True, axis_index_groups=halves
            )
            return value.reshape(rows.shape)

        spread = pl.pallas_call(
            half_norm_kernel,
            out_shape=rows,
            in_specs=[VMEM] * 2 + [ANY] * 3,
            out_specs=VMEM,
            compiler_params=PARAMS,
            name="half_spread_normed",
        )(current, mod, packed, aux, their_aux)
        partial_value = pl.pallas_call(
            functools.partial(half_block_kernel, qkv_cols),
            out_shape=rows,
            in_specs=[VMEM] * 2 + [ANY] + [VMEM] * 2,
            out_specs=VMEM,
            scratch_shapes=[
                pltpu.VMEM(packed.shape, BF16),
                pltpu.VMEM((folded[1] // LANES, rows.shape[0], LANES), jnp.float32),
                pltpu.VMEM((window[0], width), BF16),
                pltpu.SemaphoreType.DMA((2,)),
            ],
            compiler_params=pltpu.CompilerParams(vmem_limit_bytes=24 * 1024 * 1024),
            name="half_heads_and_units",
        )(
            exchange(spread),
            pltpu.with_memory_space_constraint(packed, pltpu.VMEM),
            their_packed,
            aux,
            their_aux,
        )
        return pl.pallas_call(
            sum_kernel,
            out_shape=jax.ShapeDtypeStruct(folded, BF16),
            in_specs=[VMEM] * 3,
            out_specs=VMEM,
            compiler_params=PARAMS,
            name="half_add_shares",
        )(exchange(partial_value), current, mod)

    def turn(chip, current):
        current = when(2 * chip + 1, current, first_held)
        return when(2 * chip + 1, current, own_held)

    def late_turn(chip, current):
        for held in (first_half, own_half):
            current = lax.cond(
                section_index == 2 * chip + 1, half_step, unused(half_step), current, *held
            )
        return current

    onward = [(2 * chip + 1, 2 * chip + 3) for chip in range(1, early - 1)]
    current = lax.fori_loop(
        1, early - 1, lambda chip, rows: hand_over(turn(chip, rows), onward), current
    )
    current = turn(early - 1, current)

    current = pl.pallas_call(
        same_kernel,
        out_shape=pltpu.VMEM(current.shape, BF16),
        in_specs=[VMEM],
        out_specs=VMEM,
        compiler_params=PARAMS,
        name="rows_so_far",
    )(current)

    def from_owners(value, step):
        received = []
        for half in range(2):
            pairs = []
            for seat in range(8):
                owner = (half * SECOND + seat * HELD) // own_rows + step
                pairs.append(
                    (
                        (2 * early - 1) * req_count + owner,
                        (2 * early + 1) * req_count + 8 * half + seat,
                    )
                )
            received.append(lax.ppermute(value, AXES, pairs))
        return jnp.where(req_index < 8, received[0], received[1])

    current = pl.pallas_call(
        fold_kernel,
        out_shape=jax.ShapeDtypeStruct(folded, BF16),
        in_specs=[near, VMEM, VMEM],
        out_specs=VMEM,
        compiler_params=PARAMS,
        name="fold_rows",
    )(req_id, from_owners(current, 0), from_owners(current, 1))
    onward_late = [
        [(2 * chip + 1, 2 * chip + 3) for chip in range(first, section_count // 2 - 1, 2)]
        for first in (early, early + 1)
    ]

    def two_late_chips(step, current):
        chip = early + 2 * step
        current = hand_over(late_turn(chip, current), onward_late[0])
        current = late_turn(chip + 1, current)
        return jnp.where(
            section_index == section_count - 1, current, hand_over(current, onward_late[1])
        )

    current = lax.fori_loop(0, (section_count // 2 - early) // 2, two_late_chips, current)
    rows = pl.pallas_call(
        unfold_kernel,
        out_shape=jax.ShapeDtypeStruct((16, width), BF16),
        in_specs=[VMEM],
        out_specs=VMEM,
        compiler_params=PARAMS,
        name="unfold_rows",
    )(current)
    columns = width // section_count
    rows = rows.reshape(16, section_count, columns).swapaxes(0, 1)
    rows = lax.all_to_all(rows, "section", split_axis=0, concat_axis=0, tiled=True)
    placed = pl.pallas_call(
        place_kernel,
        out_shape=jax.ShapeDtypeStruct((patches, columns), BF16),
        in_specs=[near, VMEM, VMEM],
        out_specs=VMEM,
        compiler_params=PARAMS,
        name="place_rows",
    )(req_id, rows[section_count - 1], request_len.reshape(1, -1))
    placed = placed.reshape(req_count, own_rows, columns)
    placed = lax.all_to_all(placed, "req", split_axis=0, concat_axis=0, tiled=True)
    return jnp.sum(placed.astype(jnp.float32), axis=0).astype(BF16)


def solution(mesh):
    in_specs = (
        P("req", None),
        P(),
        P(),
        P(),
        P("section", None, None, None),
        P("section", None, "req", None),
        P("section", None, "req"),
        P("section", "req", None, None),
        P("section", "req", None),
        P("section", None, "req", None),
    )
    out_specs = P("req", "section")
    return jax.shard_map(shards, mesh=mesh, in_specs=in_specs, out_specs=out_specs, check_vma=False)
```

```python
import functools

import jax
import jax.numpy as jnp
from jax import lax
from jax.experimental import pallas as pl
from jax.experimental.pallas import tpu as pltpu
from jax.sharding import PartitionSpec as P

AXES = ("section", "req")
BF16 = jnp.bfloat16
WIDTH_CUTS = 4
TILE = 16
HELD = 10
LANES = 128
SECOND = 48
VMEM = pl.BlockSpec(memory_space=pltpu.VMEM)
ANY = pl.BlockSpec(memory_space=pl.ANY)
LARGE = pltpu.CompilerParams(vmem_limit_bytes=58 * 1024 * 1024)
PARAMS = pltpu.CompilerParams(vmem_limit_bytes=16 * 1024 * 1024)


def gelu_tanh(values):
    return (
        0.5
        * values
        * (1.0 + jnp.tanh(0.7978845608028654 * (values + 0.044715 * values * values * values)))
    )


def down(rows, cols):
    return lax.broadcasted_iota(jnp.int32, (rows, cols), 0)


def along(rows, cols):
    return lax.broadcasted_iota(jnp.int32, (rows, cols), 1)


def total(mask, values, axis):
    return jnp.sum(jnp.where(mask, values, 0.0), axis=axis, keepdims=True)


def request_starts(len_ref):
    reqs = len_ref.shape[1]
    lens = jnp.broadcast_to(len_ref[...].astype(jnp.float32), (reqs, reqs))
    lens_down = total(down(reqs, reqs) == along(reqs, reqs), lens, 1)
    return (
        total(down(reqs, reqs) < along(reqs, reqs), lens_down, 0),
        total(along(reqs, reqs) < down(reqs, reqs), lens, 1),
    )


def write_aux(aux_ref, row_of, span_ref, route_ref, len_ref, stale_ref):
    patches, reqs = route_ref.shape[1], len_ref.shape[1]
    rows, stale_cols = aux_ref.shape[0], stale_ref.shape[1]
    places = aux_ref.shape[1] - stale_cols
    span_rows = patches // span_ref.shape[0]
    f32 = jnp.float32
    starts_along, starts_down = request_starts(len_ref)
    row_down = row_of(down(rows, reqs)).astype(f32)
    row_along = row_of(along(reqs, places)).astype(f32)
    req_down = total(row_down >= starts_along, 1.0, 1) - 1.0
    req_along = total(row_along >= starts_down, 1.0, 0) - 1.0
    route = jnp.broadcast_to(route_ref[...], (patches, patches))
    route_down = total(down(patches, patches) == along(patches, patches), route.astype(f32), 1)
    at_position = row_of(down(rows, patches)) == jnp.broadcast_to(
        route_ref[...], (rows, patches)
    )
    position_down = total(at_position, along(rows, patches).astype(f32), 1)
    position_along = total(
        route_down == row_of(along(patches, places)).astype(f32),
        down(patches, places).astype(f32),
        0,
    )
    first_row = (span_ref[0] * span_rows).astype(f32)

    def in_first(position):
        return (position >= first_row) & (position < first_row + span_rows)

    from_stale = jnp.where(in_first(position_down), 1.0, 0.0) * jnp.where(
        in_first(position_along), 0.0, 1.0
    )
    counts = jnp.where(along(rows, places) < rows, 1.0, 0.0)
    kind = jnp.where(req_down == req_along, (1.0 + from_stale) * counts, 0.0)
    aux_ref[:, :stale_cols] = jnp.dot(
        jnp.where(at_position, 1.0, 0.0).astype(BF16),
        stale_ref[...],
        preferred_element_type=f32,
    ).astype(BF16)
    aux_ref[:, stale_cols:] = kind.astype(BF16)


def fetch(pairs, sems):
    copies = [
        pltpu.make_async_copy(source, target, sems.at[i])
        for i, (source, target) in enumerate(pairs)
    ]
    for copy in copies:
        copy.start()
    for copy in copies:
        copy.wait()


def prepare_kernel(
    req_ref,
    span_hbm,
    route_hbm,
    len_hbm,
    modulation_hbm,
    stale_hbm,
    aux_ref,
    mod_ref,
    span_ref,
    route_ref,
    len_ref,
    modulation_ref,
    stale_ref,
    sems,
):
    fetch(
        (
            (span_hbm, span_ref),
            (route_hbm, route_ref),
            (len_hbm, len_ref),
            (modulation_hbm, modulation_ref),
            (stale_hbm, stale_ref),
        ),
        sems,
    )
    write_aux(aux_ref, lambda place: place, span_ref, route_ref, len_ref, stale_ref)
    reqs, own_rows = len_ref.shape[1], mod_ref.shape[1]
    own = (down(own_rows, reqs) + req_ref[0] * own_rows).astype(jnp.float32)
    own_req = total(own >= request_starts(len_ref)[0], 1.0, 1) - 1.0
    for part in range(mod_ref.shape[0]):
        chosen = jnp.zeros(mod_ref.shape[1:], jnp.float32)
        for req in range(reqs):
            chosen = chosen + jnp.where(own_req == req, 1.0, 0.0) * modulation_ref[
                part, req : req + 1, :
            ]
        mod_ref[part] = chosen


def fold(rows):
    cols = rows[0].shape[1] // 8
    return jnp.concatenate(
        [
            jnp.concatenate([row[:, s * cols : (s + 1) * cols] for s in range(8)], axis=0)
            for row in rows
        ],
        axis=1,
    )


def prepare_half_kernel(
    req_ref,
    span_hbm,
    route_hbm,
    len_hbm,
    modulation_hbm,
    stale_hbm,
    mine_ref,
    theirs_ref,
    mod_ref,
    span_ref,
    route_ref,
    len_ref,
    modulation_ref,
    stale_ref,
    sems,
):
    fetch(
        (
            (span_hbm, span_ref),
            (route_hbm, route_ref),
            (len_hbm, len_ref),
            (modulation_hbm, modulation_ref),
            (stale_hbm, stale_ref),
        ),
        sems,
    )
    base = jnp.where(req_ref[0] >= 8, SECOND, 0)
    seat = jnp.bitwise_and(req_ref[0], 7)
    for first, aux_ref in ((base, mine_ref), (SECOND - base, theirs_ref)):

        def row_of(place):
            return first + jnp.bitwise_and(place, 7) * HELD + lax.shift_right_logical(place, 3)

        write_aux(aux_ref, row_of, span_ref, route_ref, len_ref, stale_ref)
    reqs = len_ref.shape[1]
    held = (down(16, reqs) + base + seat * HELD).astype(jnp.float32)
    held_req = total(held >= request_starts(len_ref)[0], 1.0, 1) - 1.0
    for part in range(mod_ref.shape[0]):
        chosen = jnp.zeros((16, modulation_ref.shape[2]), jnp.float32)
        for req in range(reqs):
            chosen = chosen + jnp.where(held_req == req, 1.0, 0.0) * modulation_ref[
                part, req : req + 1, :
            ]
        mod_ref[part] = fold([chosen[i : i + 1] for i in range(HELD)])


def same_kernel(values_ref, out_ref):
    out_ref[...] = values_ref[...]


def fold_kernel(req_ref, first_ref, second_ref, out_ref):
    skipped = jnp.bitwise_and(jnp.bitwise_and(req_ref[0], 7) * HELD, 7)
    rows = jnp.concatenate(
        [first_ref[...].astype(jnp.float32), second_ref[...].astype(jnp.float32)], axis=0
    ).astype(BF16)
    pick = jnp.where(along(16, 16) == down(16, 16) + skipped, 1.0, 0.0).astype(BF16)
    picked = jnp.dot(pick, rows, preferred_element_type=jnp.float32)
    out_ref[...] = fold([picked[i : i + 1] for i in range(HELD)]).astype(BF16)


def unfold_kernel(current_ref, out_ref):
    cols = current_ref.shape[1] // HELD
    current = current_ref[...].astype(jnp.float32)
    rows = [
        jnp.concatenate(
            [current[s : s + 1, i * cols : (i + 1) * cols] for s in range(8)], axis=1
        )
        for i in range(HELD)
    ]
    rows.append(jnp.zeros((out_ref.shape[0] - HELD, 8 * cols), jnp.float32))
    out_ref[...] = jnp.concatenate(rows, axis=0).astype(BF16)


def place_kernel(req_ref, rows_ref, len_ref, out_ref):
    patches, held = out_ref.shape[0], rows_ref.shape[0]
    base = jnp.where(req_ref[0] >= 8, SECOND, 0)
    held_first = base + jnp.bitwise_and(req_ref[0], 7) * HELD
    starts, _ = request_starts(len_ref)
    ends = starts + len_ref[...].astype(jnp.float32)
    border = jnp.max(jnp.where(ends <= 8 * HELD, ends, 0.0), axis=1, keepdims=True)
    place = down(patches, held)
    before = place.astype(jnp.float32) < border
    first_half = jnp.where(base == 0, 1.0, 0.0)
    counts = jnp.where(before, first_half, 1.0 - first_half)
    here = jnp.where(
        (place == held_first + along(patches, held)) & (along(patches, held) < HELD), counts, 0.0
    )
    out_ref[...] = jnp.dot(
        here.astype(BF16), rows_ref[...], preferred_element_type=jnp.float32
    ).astype(BF16)


def pack_kernel(qkv_ref, mlp_ref, attn_out_ref, mlp_out_ref, packed_ref, sems):
    width, qkv_cols = qkv_ref.shape
    head_dim, units = attn_out_ref.shape[0], mlp_out_ref.shape[0]
    cols = packed_ref.shape[1]
    moves = [
        (qkv_ref, packed_ref.at[pl.ds(0, width), pl.ds(0, qkv_cols)]),
        (mlp_ref, packed_ref.at[pl.ds(0, width), pl.ds(qkv_cols, units)]),
    ]
    for cut in range(width // cols):
        first = width + cut * (head_dim + units)
        span = pl.ds(cut * cols, cols)
        moves += [
            (attn_out_ref.at[:, span], packed_ref.at[pl.ds(first, head_dim), :]),
            (mlp_out_ref.at[:, span], packed_ref.at[pl.ds(first + head_dim, units), :]),
        ]
    copies = [
        pltpu.make_async_copy(source, target, sems.at[i])
        for i, (source, target) in enumerate(moves)
    ]
    for copy in copies:
        copy.start()
    for copy in copies:
        copy.wait()


def attend(qkv, aux_ref):
    head_dim = qkv.shape[1] // 3
    rows = qkv.shape[0]
    stale_cols = 2 * head_dim
    places = aux_ref.shape[1] - stale_cols

    def both_kinds(fresh, stale):
        if rows == places:
            return jnp.concatenate([fresh, stale], axis=0)
        none = jnp.zeros((places - rows, head_dim), BF16)
        return jnp.concatenate([fresh, none, stale, none], axis=0)

    query = qkv[:, :head_dim]
    keys = both_kinds(qkv[:, head_dim:stale_cols], aux_ref[:, :head_dim])
    values = both_kinds(qkv[:, stale_cols:], aux_ref[:, head_dim:stale_cols])
    kind = aux_ref[:, stale_cols:].astype(jnp.float32)
    from_stale = kind > 1.5
    both = lax.dot_general(
        query, keys, (((1,), (1,)), ((), ())), preferred_element_type=jnp.float32
    )
    scores = jnp.where(from_stale, both[:, places:], both[:, :places]) / jnp.sqrt(
        jnp.float32(head_dim)
    )
    scores = jnp.where(kind > 0.5, scores, -jnp.inf)
    exps = jnp.exp(scores - jnp.max(scores, axis=-1, keepdims=True))
    weights = jnp.concatenate(
        [jnp.where(from_stale, 0.0, exps), jnp.where(from_stale, exps, 0.0)], axis=1
    ).astype(BF16)
    attended = jnp.dot(weights, values, preferred_element_type=jnp.float32)
    return (attended / jnp.sum(exps, axis=-1, keepdims=True)).astype(BF16)


def block_kernel(
    rows_ref,
    qkv_ref,
    mlp_ref,
    attn_out_ref,
    mlp_out_ref,
    aux_ref,
    out_ref,
):
    qkv = jnp.dot(rows_ref[...], qkv_ref[...], preferred_element_type=jnp.float32).astype(BF16)
    attended = attend(qkv, aux_ref)
    mlp_act = gelu_tanh(
        jnp.dot(rows_ref[...], mlp_ref[...], preferred_element_type=jnp.float32)
    ).astype(BF16)
    cols = out_ref.shape[1] // WIDTH_CUTS
    for cut in range(WIDTH_CUTS):
        span = slice(cut * cols, (cut + 1) * cols)
        out_ref[:, span] = (
            jnp.dot(attended, attn_out_ref[:, span], preferred_element_type=jnp.float32)
            + jnp.dot(mlp_act, mlp_out_ref[:, span], preferred_element_type=jnp.float32)
        ).astype(BF16)


def packed_block_kernel(qkv_cols, rows_ref, packed_ref, aux_ref, out_ref):
    width = rows_ref.shape[1]
    cols = packed_ref.shape[1]
    cuts = width // cols
    depth = (packed_ref.shape[0] - width) // cuts
    total = jnp.dot(
        rows_ref[...], packed_ref[:width, :], preferred_element_type=jnp.float32
    )
    attended = attend(total[:, :qkv_cols].astype(BF16), aux_ref)
    mlp_act = gelu_tanh(total[:, qkv_cols:]).astype(BF16)
    inner = jnp.concatenate([attended, mlp_act], axis=1)
    for cut in range(cuts):
        first = width + cut * depth
        out_ref[:, cut * cols : (cut + 1) * cols] = jnp.dot(
            inner, packed_ref[first : first + depth, :], preferred_element_type=jnp.float32
        ).astype(BF16)


def half_block_kernel(
    qkv_cols,
    rows_ref,
    packed_ref,
    their_packed_hbm,
    aux_ref,
    their_aux_ref,
    out_ref,
    their_packed_ref,
    spread_ref,
    inputs_ref,
    sems,
):
    width = inputs_ref.shape[1]
    rest = packed_ref.shape[0] - width
    reads = [
        pltpu.make_async_copy(
            their_packed_hbm.at[pl.ds(first, count), :],
            their_packed_ref.at[pl.ds(first, count), :],
            sems.at[i],
        )
        for i, (first, count) in enumerate(((0, width), (width, rest)))
    ]
    for read in reads:
        read.start()
    piece = width // 8
    cols = packed_ref.shape[1]
    cuts = width // cols
    depth = (packed_ref.shape[0] - width) // cuts
    tiles = piece // LANES
    for tile in range(spread_ref.shape[0]):
        spread_ref[tile] = rows_ref[:, tile * LANES : (tile + 1) * LANES].astype(jnp.float32)
    for i in range(0, HELD, 2):
        for s in range(8):
            for t in range(tiles):
                inputs_ref[
                    8 * i : 8 * i + 16, s * piece + t * LANES : s * piece + (t + 1) * LANES
                ] = jnp.concatenate(
                    [spread_ref[k * tiles + t, pl.ds(s, 8, stride=8), :] for k in (i, i + 1)],
                    axis=0,
                ).astype(BF16)
    def inner_of(weights, extra):
        sums = jnp.dot(
            inputs_ref[...], weights[:width, :], preferred_element_type=jnp.float32
        )
        attended = attend(sums[:, :qkv_cols].astype(BF16), extra)
        mlp_act = gelu_tanh(sums[:, qkv_cols:]).astype(BF16)
        return jnp.concatenate([attended, mlp_act], axis=1)

    inner = [inner_of(packed_ref, aux_ref)]
    reads[0].wait()
    inner.append(inner_of(their_packed_ref, their_aux_ref))
    reads[1].wait()
    for cut in range(cuts):
        first = width + cut * depth
        out = jnp.dot(
            inner[0], packed_ref[first : first + depth, :], preferred_element_type=jnp.float32
        ) + jnp.dot(
            inner[1],
            their_packed_ref[first : first + depth, :],
            preferred_element_type=jnp.float32,
        )
        for k in range(cols // piece):
            s = cut * (cols // piece) + k
            for i in range(HELD):
                for t in range(tiles):
                    first = k * piece + t * LANES
                    spread_ref[i * tiles + t, pl.ds(s, 8, stride=8), :] = out[
                        8 * i : 8 * i + 8, first : first + LANES
                    ]
    for tile in range(spread_ref.shape[0]):
        out_ref[:, tile * LANES : (tile + 1) * LANES] = spread_ref[tile].astype(BF16)


def of_row(values):
    return jnp.sum(jnp.sum(values, axis=1, keepdims=True), axis=0, keepdims=True)


def half_norm_kernel(current_ref, mod_ref, *refs):
    out_ref = refs[-1]
    current = current_ref[...].astype(jnp.float32)
    cols = current.shape[1] // HELD
    normed = []
    for i in range(HELD):
        values = current[:, i * cols : (i + 1) * cols]
        centered = values - of_row(values) / (8 * cols)
        normed.append(centered * lax.rsqrt(of_row(centered * centered) / (8 * cols) + 1e-06))
    normed = jnp.concatenate(normed, axis=1) * (1.0 + mod_ref[1]) + mod_ref[0]
    twice = jnp.concatenate([normed, normed], axis=0).astype(BF16)
    for first in range(0, out_ref.shape[0], TILE):
        out_ref[first : first + TILE, :] = twice


def spread_normed(current, mod_ref, out_ref):
    row_mean = jnp.mean(current, axis=-1, keepdims=True)
    centered = current - row_mean
    row_var = jnp.mean(centered * centered, axis=-1, keepdims=True)
    normed = centered * lax.rsqrt(row_var + 1e-06) * (1.0 + mod_ref[1]) + mod_ref[0]
    twice = jnp.concatenate([normed, normed], axis=0).astype(BF16)
    for first in range(0, out_ref.shape[0], TILE):
        out_ref[first : first + TILE, :] = twice


def summed(shares_ref, current_ref, mod_ref):
    branch = shares_ref[:TILE, :].astype(jnp.float32)
    for first in range(TILE, shares_ref.shape[0], TILE):
        branch = branch + shares_ref[first : first + TILE, :].astype(jnp.float32)
    branch = branch[: TILE // 2] + branch[TILE // 2 :]
    return (current_ref[...].astype(jnp.float32) + mod_ref[2] * branch).astype(BF16)


def nothing_kernel(*refs):
    pass


def keep_kernel(least, section_ref, *refs):
    *refs, sems = refs
    count = len(refs) // 2

    @pl.when(section_ref[0] >= least)
    def _():
        fetch(list(zip(refs[:count], refs[count:])), sems)


def norm_kernel(current_ref, mod_ref, *refs):
    spread_normed(current_ref[...].astype(jnp.float32), mod_ref, refs[-1])


def sum_kernel(shares_ref, current_ref, mod_ref, out_ref):
    out_ref[...] = summed(shares_ref, current_ref, mod_ref)


def shards(
    latents,
    patch_route,
    request_len,
    span_order,
    modulation,
    w_qkv,
    w_mlp_in,
    w_out_attn,
    w_out_mlp,
    stale_kv,
):
    section_count = lax.axis_size("section")
    req_count = lax.axis_size("req")
    section_index = lax.axis_index("section")
    req_index = lax.axis_index("req")
    patches = patch_route.shape[0]
    own_rows, width = latents.shape
    qkv_cols = w_qkv.shape[3]
    head_dim = w_out_attn.shape[2]
    units = w_mlp_in.shape[2]

    near = pl.BlockSpec(memory_space=pltpu.SMEM)
    operands = (
        span_order,
        patch_route.reshape(1, patches),
        request_len.reshape(1, -1),
        modulation[0].swapaxes(0, 1),
        stale_kv[0, :, 0],
    )
    aux, mod = pl.pallas_call(
        prepare_kernel,
        out_shape=(
            pltpu.VMEM((patches, 2 * head_dim + patches), BF16),
            pltpu.VMEM((3, own_rows, width), jnp.float32),
        ),
        in_specs=[near] + [ANY] * 5,
        out_specs=(VMEM, VMEM),
        scratch_shapes=[pltpu.SMEM(span_order.shape, span_order.dtype)]
        + [pltpu.VMEM(value.shape, value.dtype) for value in operands[1:]]
        + [pltpu.SemaphoreType.DMA((5,))],
        compiler_params=LARGE,
        name="prepare",
    )(req_index.astype(jnp.int32).reshape(1), *operands)
    mod, aux = lax.optimization_barrier((mod, aux))
    own_weights = (w_qkv[0, :, 0], w_mlp_in[0], w_out_attn[0, 0], w_out_mlp[0])
    to_sibling = [
        (i, i + req_count)
        for i in range(2 * req_count, section_count * req_count)
        if i // req_count % 2 == 0
    ]
    packed_cols = qkv_cols + units
    pack = pl.pallas_call(
        pack_kernel,
        out_shape=jax.ShapeDtypeStruct(
            (width + width // packed_cols * (head_dim + units), packed_cols), BF16
        ),
        in_specs=[ANY] * 4,
        out_specs=VMEM,
        compiler_params=PARAMS,
        scratch_shapes=[pltpu.SemaphoreType.DMA((2 + 2 * (width // packed_cols),))],
        name="pack_weights",
    )

    def chip_sections(weights, aux, mod):
        own = (pack(*weights), aux, mod)
        return own[0], *(lax.ppermute(value, AXES, to_sibling) for value in own)

    def unused(function):
        def nothing(*values):
            shapes, tree = jax.tree.flatten(jax.eval_shape(function, *values))
            results = pl.pallas_call(
                nothing_kernel,
                out_shape=tuple(jax.ShapeDtypeStruct(v.shape, v.dtype) for v in shapes),
                out_specs=(ANY,) * len(shapes),
                name="unused",
            )()
            return jax.tree.unflatten(tree, results)

        return nothing

    all_rows = jax.ShapeDtypeStruct((patches, width), BF16)
    own = jax.ShapeDtypeStruct((own_rows, width), BF16)
    def norm(current, mod, *weights):
        return pl.pallas_call(
            norm_kernel,
            out_shape=all_rows,
            in_specs=[VMEM] * 2 + [ANY] * len(weights),
            out_specs=VMEM,
            compiler_params=PARAMS,
            name="spread_normed",
        )(current, mod, *weights)

    def heads_and_units(everyone, weights, aux):
        kernel = block_kernel
        if len(weights) == 1:
            kernel = functools.partial(packed_block_kernel, qkv_cols)
        return pl.pallas_call(
            kernel,
            out_shape=all_rows,
            in_specs=[VMEM] * (2 + len(weights)),
            out_specs=VMEM,
            compiler_params=PARAMS,
            name="heads_and_units",
        )(
            everyone,
            *[pltpu.with_memory_space_constraint(value, pltpu.VMEM) for value in weights],
            aux,
        )

    add_shares = pl.pallas_call(
        sum_kernel,
        out_shape=own,
        in_specs=[VMEM] * 3,
        out_specs=VMEM,
        compiler_params=PARAMS,
        name="add_shares",
    )

    def exchange(value):
        value = value.reshape(req_count, own_rows, width)
        value = lax.all_to_all(value, "req", split_axis=0, concat_axis=0, tiled=True)
        return value.reshape(patches, width)

    def one_section(current, *section):
        *weights, aux, mod = section
        everyone = exchange(norm(current, mod, *weights, aux))
        partial_value = heads_and_units(everyone, weights, aux)
        return add_shares(exchange(partial_value), current, mod)

    def when(section, current, held):
        return lax.cond(
            section_index == section, one_section, unused(one_section), current, *held
        )

    def hand_over(current, sections):
        pairs = [(a * req_count + i, b * req_count + i) for a, b in sections for i in range(req_count)]
        return lax.ppermute(current, AXES, pairs)

    start = (*own_weights, aux, mod)
    current = hand_over(when(0, latents, start), [(0, 1)])
    current = hand_over(when(1, current, start), [(1, 3)])

    def settle(least, packed, small):
        packed = pl.pallas_call(
            nothing_kernel,
            out_shape=tuple(jax.ShapeDtypeStruct(value.shape, BF16) for value in packed),
            in_specs=[ANY] * len(packed),
            out_specs=(ANY,) * len(packed),
            input_output_aliases={i: i for i in range(len(packed))},
            name="pass_on",
        )(*packed)
        small = pl.pallas_call(
            functools.partial(keep_kernel, least),
            out_shape=tuple(pltpu.VMEM(value.shape, value.dtype) for value in small),
            in_specs=[near] + [ANY] * len(small),
            out_specs=(VMEM,) * len(small),
            scratch_shapes=[pltpu.SemaphoreType.DMA((len(small),))],
            compiler_params=LARGE,
            name="keep",
        )(section_index.astype(jnp.int32).reshape(1), *small)
        return packed, small

    own_packed, *first = lax.cond(
        section_index >= 2, chip_sections, unused(chip_sections), own_weights, aux, mod
    )
    (own_packed, first_packed), small = settle(2, (own_packed, first[0]), first[1:])
    first_held, own_held = (first_packed, *small), (own_packed, aux, mod)

    early = section_count // 4
    req_id = req_index.astype(jnp.int32).reshape(1)
    side = 4
    partner = [(side - 1 - r // side) * side + r % side for r in range(req_count)]
    window = (8 * HELD, 2 * head_dim + patches)
    folded = (8, HELD * width // 8)

    def late_sections(own_packed, first_packed, *operands):
        mine, theirs, mods = pl.pallas_call(
            prepare_half_kernel,
            out_shape=(
                jax.ShapeDtypeStruct(window, BF16),
                jax.ShapeDtypeStruct(window, BF16),
                jax.ShapeDtypeStruct((3, *folded), jnp.float32),
            ),
            in_specs=[near] + [ANY] * 5,
            out_specs=(VMEM,) * 3,
            scratch_shapes=[pltpu.SMEM(span_order.shape, span_order.dtype)]
            + [pltpu.VMEM(value.shape, value.dtype) for value in operands[1:]]
            + [pltpu.SemaphoreType.DMA((5,))],
            compiler_params=PARAMS,
            name="prepare_half",
        )(req_id, *operands)
        own = (mine, theirs, mods)
        pairs = [
            (i, i + req_count)
            for i in range(2 * early * req_count, section_count * req_count)
            if i // req_count % 2 == 0
        ]
        first = tuple(lax.ppermute(value, AXES, pairs) for value in own)
        swap = [
            (s * req_count + r, s * req_count + partner[r])
            for s in range(2 * early + 1, section_count, 2)
            for r in range(req_count)
        ]
        swapped = tuple(
            lax.ppermute(value, AXES, swap)
            for value in (first[1], own[1], first_packed, own_packed)
        )
        return (*swapped[2:], first[0], swapped[0], first[2], own[0], swapped[1], own[2])

    late = lax.cond(
        section_index >= 2 * early,
        late_sections,
        unused(late_sections),
        own_packed,
        first_packed,
        *operands,
    )
    their_packed, small = settle(2 * early, late[:2], late[2:])
    first_half = (first_packed, their_packed[0], *small[:3])
    own_half = (own_packed, their_packed[1], *small[3:])

    def half_step(current, packed, their_packed, aux, their_aux, mod):
        rows = jax.ShapeDtypeStruct((8 * 8, folded[1]), BF16)
        halves = [list(range(8)), list(range(8, 16))]

        def exchange(value):
            value = value.reshape(8, *folded)
            value = lax.all_to_all(
                value, "req", split_axis=0, concat_axis=0, tiled=True, axis_index_groups=halves
            )
            return value.reshape(rows.shape)

        spread = pl.pallas_call(
            half_norm_kernel,
            out_shape=rows,
            in_specs=[VMEM] * 2 + [ANY] * 3,
            out_specs=VMEM,
            compiler_params=PARAMS,
            name="half_spread_normed",
        )(current, mod, packed, aux, their_aux)
        partial_value = pl.pallas_call(
            functools.partial(half_block_kernel, qkv_cols),
            out_shape=rows,
            in_specs=[VMEM] * 2 + [ANY] + [VMEM] * 2,
            out_specs=VMEM,
            scratch_shapes=[
                pltpu.VMEM(packed.shape, BF16),
                pltpu.VMEM((folded[1] // LANES, rows.shape[0], LANES), jnp.float32),
                pltpu.VMEM((window[0], width), BF16),
                pltpu.SemaphoreType.DMA((2,)),
            ],
            compiler_params=pltpu.CompilerParams(vmem_limit_bytes=24 * 1024 * 1024),
            name="half_heads_and_units",
        )(
            exchange(spread),
            pltpu.with_memory_space_constraint(packed, pltpu.VMEM),
            their_packed,
            aux,
            their_aux,
        )
        return pl.pallas_call(
            sum_kernel,
            out_shape=jax.ShapeDtypeStruct(folded, BF16),
            in_specs=[VMEM] * 3,
            out_specs=VMEM,
            compiler_params=PARAMS,
            name="half_add_shares",
        )(exchange(partial_value), current, mod)

    def turn(chip, current):
        current = when(2 * chip + 1, current, first_held)
        return when(2 * chip + 1, current, own_held)

    def late_turn(chip, current):
        for held in (first_half, own_half):
            current = lax.cond(
                section_index == 2 * chip + 1, half_step, unused(half_step), current, *held
            )
        return current

    onward = [(2 * chip + 1, 2 * chip + 3) for chip in range(1, early - 1)]
    current = lax.fori_loop(
        1, early - 1, lambda chip, rows: hand_over(turn(chip, rows), onward), current
    )
    current = turn(early - 1, current)

    current = pl.pallas_call(
        same_kernel,
        out_shape=pltpu.VMEM(current.shape, BF16),
        in_specs=[VMEM],
        out_specs=VMEM,
        compiler_params=PARAMS,
        name="rows_so_far",
    )(current)

    def from_owners(value, step):
        received = []
        for half in range(2):
            pairs = []
            for seat in range(8):
                owner = (half * SECOND + seat * HELD) // own_rows + step
                pairs.append(
                    (
                        (2 * early - 1) * req_count + owner,
                        (2 * early + 1) * req_count + 8 * half + seat,
                    )
                )
            received.append(lax.ppermute(value, AXES, pairs))
        return jnp.where(req_index < 8, received[0], received[1])

    current = pl.pallas_call(
        fold_kernel,
        out_shape=jax.ShapeDtypeStruct(folded, BF16),
        in_specs=[near, VMEM, VMEM],
        out_specs=VMEM,
        compiler_params=PARAMS,
        name="fold_rows",
    )(req_id, from_owners(current, 0), from_owners(current, 1))
    onward_late = [
        [(2 * chip + 1, 2 * chip + 3) for chip in range(first, section_count // 2 - 1, 2)]
        for first in (early, early + 1)
    ]

    def two_late_chips(step, current):
        chip = early + 2 * step
        current = hand_over(late_turn(chip, current), onward_late[0])
        current = late_turn(chip + 1, current)
        return jnp.where(
            section_index == section_count - 1, current, hand_over(current, onward_late[1])
        )

    current = lax.fori_loop(0, (section_count // 2 - early) // 2, two_late_chips, current)
    rows = pl.pallas_call(
        unfold_kernel,
        out_shape=jax.ShapeDtypeStruct((16, width), BF16),
        in_specs=[VMEM],
        out_specs=VMEM,
        compiler_params=PARAMS,
        name="unfold_rows",
    )(current)
    columns = width // section_count
    rows = rows.reshape(16, section_count, columns).swapaxes(0, 1)
    rows = lax.all_to_all(rows, "section", split_axis=0, concat_axis=0, tiled=True)
    placed = pl.pallas_call(
        place_kernel,
        out_shape=jax.ShapeDtypeStruct((patches, columns), BF16),
        in_specs=[near, VMEM, VMEM],
        out_specs=VMEM,
        compiler_params=PARAMS,
        name="place_rows",
    )(req_id, rows[section_count - 1], request_len.reshape(1, -1))
    placed = placed.reshape(req_count, own_rows, columns)
    placed = lax.all_to_all(placed, "req", split_axis=0, concat_axis=0, tiled=True)
    return jnp.sum(placed.astype(jnp.float32), axis=0).astype(BF16)


def solution(mesh):
    in_specs = (
        P("req", None),
        P(),
        P(),
        P(),
        P("section", None, None, None),
        P("section", None, "req", None),
        P("section", None, "req"),
        P("section", "req", None, None),
        P("section", "req", None),
        P("section", None, "req", None),
    )
    out_specs = P("req", "section")
    return jax.shard_map(shards, mesh=mesh, in_specs=in_specs, out_specs=out_specs, check_vma=False)
```

```python
import functools

import jax
import jax.numpy as jnp
from jax import lax
from jax.experimental import pallas as pl
from jax.experimental.pallas import tpu as pltpu
from jax.sharding import PartitionSpec as P

AXES = ("section", "req")
BF16 = jnp.bfloat16
WIDTH_CUTS = 4
TILE = 16
HELD = 10
LANES = 128
SECOND = 48
VMEM = pl.BlockSpec(memory_space=pltpu.VMEM)
ANY = pl.BlockSpec(memory_space=pl.ANY)
LARGE = pltpu.CompilerParams(vmem_limit_bytes=58 * 1024 * 1024)
PARAMS = pltpu.CompilerParams(vmem_limit_bytes=16 * 1024 * 1024)


def gelu_tanh(values):
    return (
        0.5
        * values
        * (1.0 + jnp.tanh(0.7978845608028654 * (values + 0.044715 * values * values * values)))
    )


def down(rows, cols):
    return lax.broadcasted_iota(jnp.int32, (rows, cols), 0)


def along(rows, cols):
    return lax.broadcasted_iota(jnp.int32, (rows, cols), 1)


def total(mask, values, axis):
    return jnp.sum(jnp.where(mask, values, 0.0), axis=axis, keepdims=True)


def request_starts(len_ref):
    reqs = len_ref.shape[1]
    lens = jnp.broadcast_to(len_ref[...].astype(jnp.float32), (reqs, reqs))
    lens_down = total(down(reqs, reqs) == along(reqs, reqs), lens, 1)
    return (
        total(down(reqs, reqs) < along(reqs, reqs), lens_down, 0),
        total(along(reqs, reqs) < down(reqs, reqs), lens, 1),
    )


def write_aux(aux_ref, row_of, span_ref, route_ref, len_ref, stale_ref):
    patches, reqs = route_ref.shape[1], len_ref.shape[1]
    rows, stale_cols = aux_ref.shape[0], stale_ref.shape[1]
    places = aux_ref.shape[1] - stale_cols
    span_rows = patches // span_ref.shape[0]
    f32 = jnp.float32
    starts_along, starts_down = request_starts(len_ref)
    row_down = row_of(down(rows, reqs)).astype(f32)
    row_along = row_of(along(reqs, places)).astype(f32)
    req_down = total(row_down >= starts_along, 1.0, 1) - 1.0
    req_along = total(row_along >= starts_down, 1.0, 0) - 1.0
    route = jnp.broadcast_to(route_ref[...], (patches, patches))
    route_down = total(down(patches, patches) == along(patches, patches), route.astype(f32), 1)
    at_position = row_of(down(rows, patches)) == jnp.broadcast_to(
        route_ref[...], (rows, patches)
    )
    position_down = total(at_position, along(rows, patches).astype(f32), 1)
    position_along = total(
        route_down == row_of(along(patches, places)).astype(f32),
        down(patches, places).astype(f32),
        0,
    )
    first_row = (span_ref[0] * span_rows).astype(f32)

    def in_first(position):
        return (position >= first_row) & (position < first_row + span_rows)

    from_stale = jnp.where(in_first(position_down), 1.0, 0.0) * jnp.where(
        in_first(position_along), 0.0, 1.0
    )
    counts = jnp.where(along(rows, places) < rows, 1.0, 0.0)
    kind = jnp.where(req_down == req_along, (1.0 + from_stale) * counts, 0.0)
    aux_ref[:, :stale_cols] = jnp.dot(
        jnp.where(at_position, 1.0, 0.0).astype(BF16),
        stale_ref[...],
        preferred_element_type=f32,
    ).astype(BF16)
    aux_ref[:, stale_cols:] = kind.astype(BF16)


def fetch(pairs, sems):
    copies = [
        pltpu.make_async_copy(source, target, sems.at[i])
        for i, (source, target) in enumerate(pairs)
    ]
    for copy in copies:
        copy.start()
    for copy in copies:
        copy.wait()


def prepare_kernel(
    req_ref,
    span_hbm,
    route_hbm,
    len_hbm,
    modulation_hbm,
    stale_hbm,
    aux_ref,
    mod_ref,
    span_ref,
    route_ref,
    len_ref,
    modulation_ref,
    stale_ref,
    sems,
):
    fetch(
        (
            (span_hbm, span_ref),
            (route_hbm, route_ref),
            (len_hbm, len_ref),
            (modulation_hbm, modulation_ref),
            (stale_hbm, stale_ref),
        ),
        sems,
    )
    write_aux(aux_ref, lambda place: place, span_ref, route_ref, len_ref, stale_ref)
    reqs, own_rows = len_ref.shape[1], mod_ref.shape[1]
    own = (down(own_rows, reqs) + req_ref[0] * own_rows).astype(jnp.float32)
    own_req = total(own >= request_starts(len_ref)[0], 1.0, 1) - 1.0
    for part in range(mod_ref.shape[0]):
        chosen = jnp.zeros(mod_ref.shape[1:], jnp.float32)
        for req in range(reqs):
            chosen = chosen + jnp.where(own_req == req, 1.0, 0.0) * modulation_ref[
                part, req : req + 1, :
            ]
        mod_ref[part] = chosen


def fold(rows):
    cols = rows[0].shape[1] // 8
    return jnp.concatenate(
        [
            jnp.concatenate([row[:, s * cols : (s + 1) * cols] for s in range(8)], axis=0)
            for row in rows
        ],
        axis=1,
    )


def prepare_half_kernel(
    req_ref,
    span_hbm,
    route_hbm,
    len_hbm,
    modulation_hbm,
    stale_hbm,
    mine_ref,
    theirs_ref,
    mod_ref,
    span_ref,
    route_ref,
    len_ref,
    modulation_ref,
    stale_ref,
    sems,
):
    fetch(
        (
            (span_hbm, span_ref),
            (route_hbm, route_ref),
            (len_hbm, len_ref),
            (modulation_hbm, modulation_ref),
            (stale_hbm, stale_ref),
        ),
        sems,
    )
    base = jnp.where(req_ref[0] >= 8, SECOND, 0)
    seat = jnp.bitwise_and(req_ref[0], 7)
    for first, aux_ref in ((base, mine_ref), (SECOND - base, theirs_ref)):

        def row_of(place):
            return first + jnp.bitwise_and(place, 7) * HELD + lax.shift_right_logical(place, 3)

        write_aux(aux_ref, row_of, span_ref, route_ref, len_ref, stale_ref)
    reqs = len_ref.shape[1]
    held = (down(16, reqs) + base + seat * HELD).astype(jnp.float32)
    held_req = total(held >= request_starts(len_ref)[0], 1.0, 1) - 1.0
    for part in range(mod_ref.shape[0]):
        chosen = jnp.zeros((16, modulation_ref.shape[2]), jnp.float32)
        for req in range(reqs):
            chosen = chosen + jnp.where(held_req == req, 1.0, 0.0) * modulation_ref[
                part, req : req + 1, :
            ]
        mod_ref[part] = fold([chosen[i : i + 1] for i in range(HELD)])


def same_kernel(values_ref, out_ref):
    out_ref[...] = values_ref[...]


def fold_kernel(req_ref, first_ref, second_ref, out_ref):
    skipped = jnp.bitwise_and(jnp.bitwise_and(req_ref[0], 7) * HELD, 7)
    rows = jnp.concatenate(
        [first_ref[...].astype(jnp.float32), second_ref[...].astype(jnp.float32)], axis=0
    ).astype(BF16)
    pick = jnp.where(along(16, 16) == down(16, 16) + skipped, 1.0, 0.0).astype(BF16)
    picked = jnp.dot(pick, rows, preferred_element_type=jnp.float32)
    out_ref[...] = fold([picked[i : i + 1] for i in range(HELD)]).astype(BF16)


def unfold_kernel(current_ref, out_ref):
    cols = current_ref.shape[1] // HELD
    current = current_ref[...].astype(jnp.float32)
    rows = [
        jnp.concatenate(
            [current[s : s + 1, i * cols : (i + 1) * cols] for s in range(8)], axis=1
        )
        for i in range(HELD)
    ]
    rows.append(jnp.zeros((out_ref.shape[0] - HELD, 8 * cols), jnp.float32))
    out_ref[...] = jnp.concatenate(rows, axis=0).astype(BF16)


def place_kernel(req_ref, rows_ref, len_ref, out_ref):
    patches, held = out_ref.shape[0], rows_ref.shape[0]
    base = jnp.where(req_ref[0] >= 8, SECOND, 0)
    held_first = base + jnp.bitwise_and(req_ref[0], 7) * HELD
    starts, _ = request_starts(len_ref)
    ends = starts + len_ref[...].astype(jnp.float32)
    border = jnp.max(jnp.where(ends <= 8 * HELD, ends, 0.0), axis=1, keepdims=True)
    place = down(patches, held)
    before = place.astype(jnp.float32) < border
    first_half = jnp.where(base == 0, 1.0, 0.0)
    counts = jnp.where(before, first_half, 1.0 - first_half)
    here = jnp.where(
        (place == held_first + along(patches, held)) & (along(patches, held) < HELD), counts, 0.0
    )
    out_ref[...] = jnp.dot(
        here.astype(BF16), rows_ref[...], preferred_element_type=jnp.float32
    ).astype(BF16)


def pack_kernel(qkv_ref, mlp_ref, attn_out_ref, mlp_out_ref, packed_ref, sems):
    width, qkv_cols = qkv_ref.shape
    head_dim, units = attn_out_ref.shape[0], mlp_out_ref.shape[0]
    cols = packed_ref.shape[1]
    moves = [
        (qkv_ref, packed_ref.at[pl.ds(0, width), pl.ds(0, qkv_cols)]),
        (mlp_ref, packed_ref.at[pl.ds(0, width), pl.ds(qkv_cols, units)]),
    ]
    for cut in range(width // cols):
        first = width + cut * (head_dim + units)
        span = pl.ds(cut * cols, cols)
        moves += [
            (attn_out_ref.at[:, span], packed_ref.at[pl.ds(first, head_dim), :]),
            (mlp_out_ref.at[:, span], packed_ref.at[pl.ds(first + head_dim, units), :]),
        ]
    copies = [
        pltpu.make_async_copy(source, target, sems.at[i])
        for i, (source, target) in enumerate(moves)
    ]
    for copy in copies:
        copy.start()
    for copy in copies:
        copy.wait()


def attend(qkv, aux_ref):
    head_dim = qkv.shape[1] // 3
    rows = qkv.shape[0]
    stale_cols = 2 * head_dim
    places = aux_ref.shape[1] - stale_cols

    def both_kinds(fresh, stale):
        if rows == places:
            return jnp.concatenate([fresh, stale], axis=0)
        none = jnp.zeros((places - rows, head_dim), BF16)
        return jnp.concatenate([fresh, none, stale, none], axis=0)

    query = qkv[:, :head_dim]
    keys = both_kinds(qkv[:, head_dim:stale_cols], aux_ref[:, :head_dim])
    values = both_kinds(qkv[:, stale_cols:], aux_ref[:, head_dim:stale_cols])
    kind = aux_ref[:, stale_cols:].astype(jnp.float32)
    from_stale = kind > 1.5
    both = lax.dot_general(
        query, keys, (((1,), (1,)), ((), ())), preferred_element_type=jnp.float32
    )
    scores = jnp.where(from_stale, both[:, places:], both[:, :places]) / jnp.sqrt(
        jnp.float32(head_dim)
    )
    scores = jnp.where(kind > 0.5, scores, -jnp.inf)
    exps = jnp.exp(scores - jnp.max(scores, axis=-1, keepdims=True))
    weights = jnp.concatenate(
        [jnp.where(from_stale, 0.0, exps), jnp.where(from_stale, exps, 0.0)], axis=1
    ).astype(BF16)
    attended = jnp.dot(weights, values, preferred_element_type=jnp.float32)
    return (attended / jnp.sum(exps, axis=-1, keepdims=True)).astype(BF16)


def block_kernel(
    rows_ref,
    qkv_ref,
    mlp_ref,
    attn_out_ref,
    mlp_out_ref,
    aux_ref,
    out_ref,
):
    qkv = jnp.dot(rows_ref[...], qkv_ref[...], preferred_element_type=jnp.float32).astype(BF16)
    attended = attend(qkv, aux_ref)
    mlp_act = gelu_tanh(
        jnp.dot(rows_ref[...], mlp_ref[...], preferred_element_type=jnp.float32)
    ).astype(BF16)
    cols = out_ref.shape[1] // WIDTH_CUTS
    for cut in range(WIDTH_CUTS):
        span = slice(cut * cols, (cut + 1) * cols)
        out_ref[:, span] = (
            jnp.dot(attended, attn_out_ref[:, span], preferred_element_type=jnp.float32)
            + jnp.dot(mlp_act, mlp_out_ref[:, span], preferred_element_type=jnp.float32)
        ).astype(BF16)


def packed_block_kernel(qkv_cols, rows_ref, packed_ref, aux_ref, out_ref):
    width = rows_ref.shape[1]
    cols = packed_ref.shape[1]
    cuts = width // cols
    depth = (packed_ref.shape[0] - width) // cuts
    total = jnp.dot(
        rows_ref[...], packed_ref[:width, :], preferred_element_type=jnp.float32
    )
    attended = attend(total[:, :qkv_cols].astype(BF16), aux_ref)
    mlp_act = gelu_tanh(total[:, qkv_cols:]).astype(BF16)
    inner = jnp.concatenate([attended, mlp_act], axis=1)
    for cut in range(cuts):
        first = width + cut * depth
        out_ref[:, cut * cols : (cut + 1) * cols] = jnp.dot(
            inner, packed_ref[first : first + depth, :], preferred_element_type=jnp.float32
        ).astype(BF16)


def half_block_kernel(
    qkv_cols,
    rows_ref,
    packed_ref,
    their_packed_hbm,
    aux_ref,
    their_aux_ref,
    out_ref,
    their_packed_ref,
    spread_ref,
    inputs_ref,
    sems,
):
    width = inputs_ref.shape[1]
    rest = packed_ref.shape[0] - width
    reads = [
        pltpu.make_async_copy(
            their_packed_hbm.at[pl.ds(first, count), :],
            their_packed_ref.at[pl.ds(first, count), :],
            sems.at[i],
        )
        for i, (first, count) in enumerate(((0, width), (width, rest)))
    ]
    for read in reads:
        read.start()
    piece = width // 8
    cols = packed_ref.shape[1]
    cuts = width // cols
    depth = (packed_ref.shape[0] - width) // cuts
    tiles = piece // LANES
    for tile in range(spread_ref.shape[0]):
        spread_ref[tile] = rows_ref[:, tile * LANES : (tile + 1) * LANES].astype(jnp.float32)
    for i in range(0, HELD, 2):
        for s in range(8):
            for t in range(tiles):
                inputs_ref[
                    8 * i : 8 * i + 16, s * piece + t * LANES : s * piece + (t + 1) * LANES
                ] = jnp.concatenate(
                    [spread_ref[k * tiles + t, pl.ds(s, 8, stride=8), :] for k in (i, i + 1)],
                    axis=0,
                ).astype(BF16)
    def inner_of(weights, extra):
        sums = jnp.dot(
            inputs_ref[...], weights[:width, :], preferred_element_type=jnp.float32
        )
        attended = attend(sums[:, :qkv_cols].astype(BF16), extra)
        mlp_act = gelu_tanh(sums[:, qkv_cols:]).astype(BF16)
        return jnp.concatenate([attended, mlp_act], axis=1)

    inner = [inner_of(packed_ref, aux_ref)]
    reads[0].wait()
    inner.append(inner_of(their_packed_ref, their_aux_ref))
    reads[1].wait()
    for cut in range(cuts):
        first = width + cut * depth
        out = jnp.dot(
            inner[0], packed_ref[first : first + depth, :], preferred_element_type=jnp.float32
        ) + jnp.dot(
            inner[1],
            their_packed_ref[first : first + depth, :],
            preferred_element_type=jnp.float32,
        )
        for k in range(cols // piece):
            s = cut * (cols // piece) + k
            for i in range(HELD):
                for t in range(tiles):
                    first = k * piece + t * LANES
                    spread_ref[i * tiles + t, pl.ds(s, 8, stride=8), :] = out[
                        8 * i : 8 * i + 8, first : first + LANES
                    ]
    for tile in range(spread_ref.shape[0]):
        out_ref[:, tile * LANES : (tile + 1) * LANES] = spread_ref[tile].astype(BF16)


def of_row(values):
    return jnp.sum(jnp.sum(values, axis=1, keepdims=True), axis=0, keepdims=True)


def half_norm_kernel(current_ref, mod_ref, *refs):
    out_ref = refs[-1]
    current = current_ref[...].astype(jnp.float32)
    cols = current.shape[1] // HELD
    normed = []
    for i in range(HELD):
        values = current[:, i * cols : (i + 1) * cols]
        centered = values - of_row(values) / (8 * cols)
        normed.append(centered * lax.rsqrt(of_row(centered * centered) / (8 * cols) + 1e-06))
    normed = jnp.concatenate(normed, axis=1) * (1.0 + mod_ref[1]) + mod_ref[0]
    twice = jnp.concatenate([normed, normed], axis=0).astype(BF16)
    for first in range(0, out_ref.shape[0], TILE):
        out_ref[first : first + TILE, :] = twice


def spread_normed(current, mod_ref, out_ref):
    row_mean = jnp.mean(current, axis=-1, keepdims=True)
    centered = current - row_mean
    row_var = jnp.mean(centered * centered, axis=-1, keepdims=True)
    normed = centered * lax.rsqrt(row_var + 1e-06) * (1.0 + mod_ref[1]) + mod_ref[0]
    twice = jnp.concatenate([normed, normed], axis=0).astype(BF16)
    for first in range(0, out_ref.shape[0], TILE):
        out_ref[first : first + TILE, :] = twice


def summed(shares_ref, current_ref, mod_ref):
    branch = shares_ref[:TILE, :].astype(jnp.float32)
    for first in range(TILE, shares_ref.shape[0], TILE):
        branch = branch + shares_ref[first : first + TILE, :].astype(jnp.float32)
    branch = branch[: TILE // 2] + branch[TILE // 2 :]
    return (current_ref[...].astype(jnp.float32) + mod_ref[2] * branch).astype(BF16)


def nothing_kernel(*refs):
    pass


def keep_kernel(least, section_ref, *refs):
    *refs, sems = refs
    count = len(refs) // 2

    @pl.when(section_ref[0] >= least)
    def _():
        fetch(list(zip(refs[:count], refs[count:])), sems)


def norm_kernel(current_ref, mod_ref, *refs):
    spread_normed(current_ref[...].astype(jnp.float32), mod_ref, refs[-1])


def sum_kernel(shares_ref, current_ref, mod_ref, out_ref):
    out_ref[...] = summed(shares_ref, current_ref, mod_ref)


def shards(
    latents,
    patch_route,
    request_len,
    span_order,
    modulation,
    w_qkv,
    w_mlp_in,
    w_out_attn,
    w_out_mlp,
    stale_kv,
):
    section_count = lax.axis_size("section")
    req_count = lax.axis_size("req")
    section_index = lax.axis_index("section")
    req_index = lax.axis_index("req")
    patches = patch_route.shape[0]
    own_rows, width = latents.shape
    qkv_cols = w_qkv.shape[3]
    head_dim = w_out_attn.shape[2]
    units = w_mlp_in.shape[2]

    near = pl.BlockSpec(memory_space=pltpu.SMEM)
    operands = (
        span_order,
        patch_route.reshape(1, patches),
        request_len.reshape(1, -1),
        modulation[0].swapaxes(0, 1),
        stale_kv[0, :, 0],
    )
    aux, mod = pl.pallas_call(
        prepare_kernel,
        out_shape=(
            pltpu.VMEM((patches, 2 * head_dim + patches), BF16),
            pltpu.VMEM((3, own_rows, width), jnp.float32),
        ),
        in_specs=[near] + [ANY] * 5,
        out_specs=(VMEM, VMEM),
        scratch_shapes=[pltpu.SMEM(span_order.shape, span_order.dtype)]
        + [pltpu.VMEM(value.shape, value.dtype) for value in operands[1:]]
        + [pltpu.SemaphoreType.DMA((5,))],
        compiler_params=LARGE,
        name="prepare",
    )(req_index.astype(jnp.int32).reshape(1), *operands)
    mod, aux = lax.optimization_barrier((mod, aux))
    own_weights = (w_qkv[0, :, 0], w_mlp_in[0], w_out_attn[0, 0], w_out_mlp[0])
    to_sibling = [
        (i, i + req_count)
        for i in range(2 * req_count, section_count * req_count)
        if i // req_count % 2 == 0
    ]
    packed_cols = qkv_cols + units
    pack = pl.pallas_call(
        pack_kernel,
        out_shape=jax.ShapeDtypeStruct(
            (width + width // packed_cols * (head_dim + units), packed_cols), BF16
        ),
        in_specs=[ANY] * 4,
        out_specs=VMEM,
        compiler_params=PARAMS,
        scratch_shapes=[pltpu.SemaphoreType.DMA((2 + 2 * (width // packed_cols),))],
        name="pack_weights",
    )

    def chip_sections(weights, aux, mod):
        own = (pack(*weights), aux, mod)
        return own[0], *(lax.ppermute(value, AXES, to_sibling) for value in own)

    def unused(function):
        def nothing(*values):
            shapes, tree = jax.tree.flatten(jax.eval_shape(function, *values))
            results = pl.pallas_call(
                nothing_kernel,
                out_shape=tuple(jax.ShapeDtypeStruct(v.shape, v.dtype) for v in shapes),
                out_specs=(ANY,) * len(shapes),
                name="unused",
            )()
            return jax.tree.unflatten(tree, results)

        return nothing

    all_rows = jax.ShapeDtypeStruct((patches, width), BF16)
    own = jax.ShapeDtypeStruct((own_rows, width), BF16)
    def norm(current, mod, *weights):
        return pl.pallas_call(
            norm_kernel,
            out_shape=all_rows,
            in_specs=[VMEM] * 2 + [ANY] * len(weights),
            out_specs=VMEM,
            compiler_params=PARAMS,
            name="spread_normed",
        )(current, mod, *weights)

    def heads_and_units(everyone, weights, aux):
        kernel = block_kernel
        if len(weights) == 1:
            kernel = functools.partial(packed_block_kernel, qkv_cols)
        return pl.pallas_call(
            kernel,
            out_shape=all_rows,
            in_specs=[VMEM] * (2 + len(weights)),
            out_specs=VMEM,
            compiler_params=PARAMS,
            name="heads_and_units",
        )(
            everyone,
            *[pltpu.with_memory_space_constraint(value, pltpu.VMEM) for value in weights],
            aux,
        )

    add_shares = pl.pallas_call(
        sum_kernel,
        out_shape=own,
        in_specs=[VMEM] * 3,
        out_specs=VMEM,
        compiler_params=PARAMS,
        name="add_shares",
    )

    def exchange(value):
        value = value.reshape(req_count, own_rows, width)
        value = lax.all_to_all(value, "req", split_axis=0, concat_axis=0, tiled=True)
        return value.reshape(patches, width)

    def one_section(current, *section):
        *weights, aux, mod = section
        everyone = exchange(norm(current, mod, *weights, aux))
        partial_value = heads_and_units(everyone, weights, aux)
        return add_shares(exchange(partial_value), current, mod)

    def when(section, current, held):
        return lax.cond(
            section_index == section, one_section, unused(one_section), current, *held
        )

    def hand_over(current, sections):
        pairs = [(a * req_count + i, b * req_count + i) for a, b in sections for i in range(req_count)]
        return lax.ppermute(current, AXES, pairs)

    start = (*own_weights, aux, mod)
    current = hand_over(when(0, latents, start), [(0, 1)])
    current = hand_over(when(1, current, start), [(1, 3)])

    def settle(least, packed, small):
        packed = pl.pallas_call(
            nothing_kernel,
            out_shape=tuple(jax.ShapeDtypeStruct(value.shape, BF16) for value in packed),
            in_specs=[ANY] * len(packed),
            out_specs=(ANY,) * len(packed),
            input_output_aliases={i: i for i in range(len(packed))},
            name="pass_on",
        )(*packed)
        small = pl.pallas_call(
            functools.partial(keep_kernel, least),
            out_shape=tuple(pltpu.VMEM(value.shape, value.dtype) for value in small),
            in_specs=[near] + [ANY] * len(small),
            out_specs=(VMEM,) * len(small),
            scratch_shapes=[pltpu.SemaphoreType.DMA((len(small),))],
            compiler_params=LARGE,
            name="keep",
        )(section_index.astype(jnp.int32).reshape(1), *small)
        return packed, small

    own_packed, *first = lax.cond(
        section_index >= 2, chip_sections, unused(chip_sections), own_weights, aux, mod
    )
    (own_packed, first_packed), small = settle(2, (own_packed, first[0]), first[1:])
    first_held, own_held = (first_packed, *small), (own_packed, aux, mod)

    early = section_count // 4
    req_id = req_index.astype(jnp.int32).reshape(1)
    side = 4
    partner = [(side - 1 - r // side) * side + r % side for r in range(req_count)]
    window = (8 * HELD, 2 * head_dim + patches)
    folded = (8, HELD * width // 8)

    def late_sections(own_packed, first_packed, *operands):
        mine, theirs, mods = pl.pallas_call(
            prepare_half_kernel,
            out_shape=(
                jax.ShapeDtypeStruct(window, BF16),
                jax.ShapeDtypeStruct(window, BF16),
                jax.ShapeDtypeStruct((3, *folded), jnp.float32),
            ),
            in_specs=[near] + [ANY] * 5,
            out_specs=(VMEM,) * 3,
            scratch_shapes=[pltpu.SMEM(span_order.shape, span_order.dtype)]
            + [pltpu.VMEM(value.shape, value.dtype) for value in operands[1:]]
            + [pltpu.SemaphoreType.DMA((5,))],
            compiler_params=PARAMS,
            name="prepare_half",
        )(req_id, *operands)
        own = (mine, theirs, mods)
        pairs = [
            (i, i + req_count)
            for i in range(2 * early * req_count, section_count * req_count)
            if i // req_count % 2 == 0
        ]
        first = tuple(lax.ppermute(value, AXES, pairs) for value in own)
        swap = [
            (s * req_count + r, s * req_count + partner[r])
            for s in range(2 * early + 1, section_count, 2)
            for r in range(req_count)
        ]
        swapped = tuple(
            lax.ppermute(value, AXES, swap)
            for value in (first[1], own[1], first_packed, own_packed)
        )
        return (*swapped[2:], first[0], swapped[0], first[2], own[0], swapped[1], own[2])

    late = lax.cond(
        section_index >= 2 * early,
        late_sections,
        unused(late_sections),
        own_packed,
        first_packed,
        *operands,
    )
    their_packed, small = settle(2 * early, late[:2], late[2:])
    first_half = (first_packed, their_packed[0], *small[:3])
    own_half = (own_packed, their_packed[1], *small[3:])

    def half_step(current, packed, their_packed, aux, their_aux, mod):
        rows = jax.ShapeDtypeStruct((8 * 8, folded[1]), BF16)
        halves = [list(range(8)), list(range(8, 16))]

        def exchange(value):
            value = value.reshape(8, *folded)
            value = lax.all_to_all(
                value, "req", split_axis=0, concat_axis=0, tiled=True, axis_index_groups=halves
            )
            return value.reshape(rows.shape)

        spread = pl.pallas_call(
            half_norm_kernel,
            out_shape=rows,
            in_specs=[VMEM] * 2 + [ANY] * 3,
            out_specs=VMEM,
            compiler_params=PARAMS,
            name="half_spread_normed",
        )(current, mod, packed, aux, their_aux)
        partial_value = pl.pallas_call(
            functools.partial(half_block_kernel, qkv_cols),
            out_shape=rows,
            in_specs=[VMEM] * 2 + [ANY] + [VMEM] * 2,
            out_specs=VMEM,
            scratch_shapes=[
                pltpu.VMEM(packed.shape, BF16),
                pltpu.VMEM((folded[1] // LANES, rows.shape[0], LANES), jnp.float32),
                pltpu.VMEM((window[0], width), BF16),
                pltpu.SemaphoreType.DMA((2,)),
            ],
            compiler_params=pltpu.CompilerParams(vmem_limit_bytes=24 * 1024 * 1024),
            name="half_heads_and_units",
        )(
            exchange(spread),
            pltpu.with_memory_space_constraint(packed, pltpu.VMEM),
            their_packed,
            aux,
            their_aux,
        )
        return pl.pallas_call(
            sum_kernel,
            out_shape=jax.ShapeDtypeStruct(folded, BF16),
            in_specs=[VMEM] * 3,
            out_specs=VMEM,
            compiler_params=PARAMS,
            name="half_add_shares",
        )(exchange(partial_value), current, mod)

    def turn(chip, current):
        current = when(2 * chip + 1, current, first_held)
        return when(2 * chip + 1, current, own_held)

    def late_turn(chip, current):
        for held in (first_half, own_half):
            current = lax.cond(
                section_index == 2 * chip + 1, half_step, unused(half_step), current, *held
            )
        return current

    for chip in range(1, early - 1):
        current = hand_over(turn(chip, current), [(2 * chip + 1, 2 * chip + 3)])
    current = turn(early - 1, current)

    current = pl.pallas_call(
        same_kernel,
        out_shape=pltpu.VMEM(current.shape, BF16),
        in_specs=[VMEM],
        out_specs=VMEM,
        compiler_params=PARAMS,
        name="rows_so_far",
    )(current)

    def from_owners(value, step):
        received = []
        for half in range(2):
            pairs = []
            for seat in range(8):
                owner = (half * SECOND + seat * HELD) // own_rows + step
                pairs.append(
                    (
                        (2 * early - 1) * req_count + owner,
                        (2 * early + 1) * req_count + 8 * half + seat,
                    )
                )
            received.append(lax.ppermute(value, AXES, pairs))
        return jnp.where(req_index < 8, received[0], received[1])

    current = pl.pallas_call(
        fold_kernel,
        out_shape=jax.ShapeDtypeStruct(folded, BF16),
        in_specs=[near, VMEM, VMEM],
        out_specs=VMEM,
        compiler_params=PARAMS,
        name="fold_rows",
    )(req_id, from_owners(current, 0), from_owners(current, 1))
    onward_late = [
        [(2 * chip + 1, 2 * chip + 3) for chip in range(first, section_count // 2 - 1, 2)]
        for first in (early, early + 1)
    ]

    def two_late_chips(step, current):
        chip = early + 2 * step
        current = hand_over(late_turn(chip, current), onward_late[0])
        current = late_turn(chip + 1, current)
        return jnp.where(
            section_index == section_count - 1, current, hand_over(current, onward_late[1])
        )

    current = lax.fori_loop(0, (section_count // 2 - early) // 2, two_late_chips, current)
    rows = pl.pallas_call(
        unfold_kernel,
        out_shape=jax.ShapeDtypeStruct((16, width), BF16),
        in_specs=[VMEM],
        out_specs=VMEM,
        compiler_params=PARAMS,
        name="unfold_rows",
    )(current)
    columns = width // section_count
    rows = rows.reshape(16, section_count, columns).swapaxes(0, 1)
    rows = lax.all_to_all(rows, "section", split_axis=0, concat_axis=0, tiled=True)
    placed = pl.pallas_call(
        place_kernel,
        out_shape=jax.ShapeDtypeStruct((patches, columns), BF16),
        in_specs=[near, VMEM, VMEM],
        out_specs=VMEM,
        compiler_params=PARAMS,
        name="place_rows",
    )(req_id, rows[section_count - 1], request_len.reshape(1, -1))
    placed = placed.reshape(req_count, own_rows, columns)
    placed = lax.all_to_all(placed, "req", split_axis=0, concat_axis=0, tiled=True)
    return jnp.sum(placed.astype(jnp.float32), axis=0).astype(BF16)


def solution(mesh):
    in_specs = (
        P("req", None),
        P(),
        P(),
        P(),
        P("section", None, None, None),
        P("section", None, "req", None),
        P("section", None, "req"),
        P("section", "req", None, None),
        P("section", "req", None),
        P("section", None, "req", None),
    )
    out_specs = P("req", "section")
    return jax.shard_map(shards, mesh=mesh, in_specs=in_specs, out_specs=out_specs, check_vma=False)
```
